128 devices in a mesh: replica: 4 (over x), section: 2 (over y_lo), tensor: 16 (over z, y_hi, core).
Axes of the slice: x: 4, y: 4 (y_hi: 2, y_lo: 2; y = y_hi * 2 + y_lo), z: 4, core: 2. Of those that a mesh axis runs over, the one named last changes fastest.
Arguments:
- boundary: bfloat16 [4, 2, 128, 4, 8192], P('replica', 'section', 'tensor'), may hold values from -6 to 6
- context: bfloat16 [4, 2, 128, 4, 4096], P('replica', 'section', None, None, 'tensor'), may hold values from -6 to 6
- weights: bfloat16 [4, 2, 4096, 8192], P('replica', 'section', 'tensor'), may hold values from -0.09375 to 0.09375
- momentum: bfloat16 [4, 2, 4096, 8192], P('replica', 'section', 'tensor'), may hold values from -0.119628906 to 0.119628906
- route: int32 [4, 2], replicated, may hold values from 0 to 3, as said below
- partner: int32 [4, 2], replicated, may hold values from 0 to 3, as said below
Outputs:
- stream_out: bfloat16 [4, 2, 128, 4, 8192], P('replica', 'section', 'tensor')
- context_grad: bfloat16 [4, 2, 128, 4, 4096], P('replica', 'section', None, None, 'tensor')
- new_weights: bfloat16 [4, 2, 4096, 8192], P('replica', 'section', 'tensor')
- new_momentum: bfloat16 [4, 2, 4096, 8192], P('replica', 'section', 'tensor')
The draws below stay inside these ranges and needn't reach their ends.
Inputs may be any that keep to these rules, and one draw needn't show every extreme that they name: `route`: every replica's section 1 takes at most 4 micro-batches, and in every draw one replica takes exactly 4. For each section s, partner[., s] is a permutation of the replicas with partner[r, s] != r, and the offsets (partner[r, s] - r) mod 4 take every value from 1 to 3.
All inputs are finite; a program needn't handle non-finite values.
Results may differ from the reference program's by a relative error of at most 0.017.
Values may be sent and summed in bfloat16 or wider, within the bound.
A program may use at most 192 MiB of HBM per device.

```python
import math
import jax
import jax.numpy as jnp
from jax import lax

D = 8192
HQ = 4096
MB = 2
CAP = 4
TOK = 128
REPL = 4
SECTIONS = 2
N_TENSOR = 16


def draw_route(key, part):
    key = jax.random.fold_in(key, 11)
    key_order, key_hot, key_offset = jax.random.split(key, 3)
    shuffled = jax.random.permutation(key_order, REPL * MB)
    hot_replica = jax.random.randint(key_hot, (), 0, REPL)
    offset = jax.random.randint(key_offset, (), 0, REPL - 1)
    position = jnp.arange(REPL * MB, dtype=jnp.int32)
    cold_replica = (hot_replica + 1 + (position - CAP + offset) % (REPL - 1)) % REPL
    destination = jnp.where(position < CAP, hot_replica, cold_replica).astype(jnp.int32)
    flat_route = jnp.zeros((REPL * MB,), jnp.int32).at[shuffled].set(destination)
    return flat_route.reshape(REPL, MB)


def draw_partner(key, part):
    key = jax.random.fold_in(key, 23)
    candidates = jnp.array([[1, 3, 0, 2], [2, 0, 3, 1], [2, 3, 1, 0], [3, 2, 0, 1]], jnp.int32)
    picks = jax.random.randint(key, (SECTIONS,), 0, 4)
    chosen = candidates[picks]
    return jnp.transpose(chosen).astype(jnp.int32)


def steps_of(own_key, shape, cuts, least, top_value):
    def one(dim, shards_of):
        steps = jax.random.uniform(jax.random.fold_in(jax.random.fold_in(own_key, 6), dim), (shards_of,), jnp.float32, least / len(cuts), top_value / len(cuts))
        return jnp.repeat(jnp.exp(steps), shape[dim] // shards_of).reshape((-1,) + (1,) * (len(shape) - dim - 1))

    gain = one(*cuts[0])
    for cut in cuts[1:]:
        gain = gain * one(*cut)
    return gain


def scatter_about(key, shape, width, limit, shards=(), kind=jnp.bfloat16):
    level = steps_of(key, shape, shards, -0.22, 0.18) if shards else 1.0
    entries = jax.random.normal(key, shape, jnp.float32) * width * level
    return jnp.minimum(jnp.maximum(entries, -limit), limit).astype(kind)


def setup_inputs(seed: int = 0) -> dict:
    streams_of = jax.random.split(jax.random.key(seed), 7)
    return {
        "boundary": scatter_about(streams_of[0], (REPL, SECTIONS, TOK, CAP, D), 1.0, 6.0, ((0, 4), (1, 2), (2, 16))),
        "context": scatter_about(streams_of[1], (REPL, SECTIONS, TOK, CAP, HQ), 1.0, 6.0, ((0, 4), (1, 2), (4, 16))),
        "weights": scatter_about(streams_of[2], (REPL, SECTIONS, HQ, D), HQ ** -0.5, 0.09375, ((0, 4), (1, 2), (2, 16))),
        "momentum": scatter_about(streams_of[3], (REPL, SECTIONS, HQ, D), 0.02, 0.119628906, ((0, 4), (1, 2), (2, 16))),
        "route": draw_route(jax.random.fold_in(streams_of[6], 71), 0),
        "partner": draw_partner(jax.random.fold_in(streams_of[6], 71), 0),
    }


ALPHA = 0.9
GAMMA = 0.5
BETA_SCALE = 0.4

def partial_sum(ctx_full, weight):
    block_width = HQ // N_TENSOR

    def accumulate(running, block_index):
        offset = block_index * block_width
        ctx_piece = lax.dynamic_slice_in_dim(ctx_full, offset, block_width, 2).astype(jnp.float32)
        w_piece = lax.dynamic_slice_in_dim(weight, offset, block_width, 0).astype(jnp.float32)
        block_term = jnp.einsum('tkh,hd->tkd', ctx_piece, w_piece).astype(jnp.bfloat16)
        return (running + block_term.astype(jnp.float32), None)
    running, _ = lax.scan(accumulate, jnp.zeros((TOK, CAP, D), jnp.float32), jnp.arange(N_TENSOR, dtype=jnp.int32))
    return running

def reference(boundary, context, weights, momentum, route, partner):
    flat_route = route.reshape(-1)
    owners = jnp.arange(REPL, dtype=jnp.int32)
    arrivals = (flat_route[None, :] == owners[:, None]).astype(jnp.int32)
    slot_index = jnp.cumsum(arrivals, axis=1) - 1
    counts = lax.optimization_barrier(jnp.sum(arrivals, axis=1))
    places = jnp.arange(CAP, dtype=jnp.int32)
    select = ((arrivals[:, None, :] == 1) & (slot_index[:, None, :] == places[None, :, None])).astype(jnp.float32)
    live_first = (places < MB)[None, :, None]
    branches = [[partial_sum(context[anchor, section_pos], weights[anchor, section_pos]) for section_pos in range(SECTIONS)] for anchor in range(REPL)]
    first_out = []
    for anchor in range(REPL):
        stream = (boundary[anchor, 0].astype(jnp.float32) + branches[anchor][0]).astype(jnp.bfloat16)
        first_out.append(jnp.where(live_first, stream, jnp.zeros_like(stream)))
    sent_rows = jnp.concatenate([stream[:, :MB] for stream in first_out], axis=1).astype(jnp.float32)
    second_out = []
    second_cot = []
    for target in range(REPL):
        arriving = jnp.einsum('kj,tjd->tkd', select[target], sent_rows)
        live_slots = (places < counts[target])[None, :, None]
        stream = (arriving + branches[target][1]).astype(jnp.bfloat16)
        second_out.append(jnp.where(live_slots, stream, jnp.zeros_like(stream)))
        second_cot.append(jnp.where(live_slots, boundary[target, 1], jnp.zeros_like(boundary[target, 1])))
    returned = jnp.zeros((TOK, REPL * MB, D), jnp.float32)
    for target in range(REPL):
        returned = returned + jnp.einsum('kj,tkd->tjd', select[target], second_cot[target].astype(jnp.float32))
    returned = returned.astype(jnp.bfloat16)
    padding = jnp.zeros((TOK, CAP - MB, D), jnp.bfloat16)
    first_cot = [jnp.concatenate([returned[:, anchor * MB:(anchor + 1) * MB], padding], axis=1) for anchor in range(REPL)]
    grad_scale = BETA_SCALE / math.sqrt(TOK * CAP)
    ctx_grads = []
    self_terms = []
    messages = []
    for anchor in range(REPL):
        ctx_row = []
        self_row = []
        message_row = []
        for section_pos in range(SECTIONS):
            cot_here = first_cot[anchor] if section_pos == 0 else second_cot[anchor]
            weight = weights[anchor, section_pos]
            ctx_row.append(jnp.einsum('tkd,hd->tkh', cot_here.astype(jnp.float32), weight.astype(jnp.float32)).astype(jnp.bfloat16))
            grad_sum = jnp.einsum('tkh,tkd->hd', context[anchor, section_pos].astype(jnp.float32), cot_here.astype(jnp.float32))
            current = weight.astype(jnp.float32)
            message_row.append((grad_scale * grad_sum - GAMMA * current).astype(jnp.bfloat16))
            self_row.append(ALPHA * momentum[anchor, section_pos].astype(jnp.float32) - 0.5 * (grad_scale * grad_sum + GAMMA * current))
        ctx_grads.append(jnp.stack(ctx_row))
        self_terms.append(self_row)
        messages.append(jnp.stack(message_row))
    messages = jnp.stack(messages)
    new_weights = []
    new_momentum = []
    for anchor in range(REPL):
        weight_row = []
        momentum_row = []
        for section_pos in range(SECTIONS):
            partner_message = messages[partner[anchor, section_pos], section_pos]
            step_delta = self_terms[anchor][section_pos] - 0.5 * partner_message.astype(jnp.float32)
            momentum_row.append(step_delta.astype(jnp.bfloat16))
            weight_row.append((weights[anchor, section_pos].astype(jnp.float32) + step_delta).astype(jnp.bfloat16))
        new_weights.append(jnp.stack(weight_row))
        new_momentum.append(jnp.stack(momentum_row))
    stream_out = jnp.stack([jnp.stack([first_out[anchor], second_out[anchor]]) for anchor in range(REPL)])
    return (stream_out, jnp.stack(ctx_grads), jnp.stack(new_weights), jnp.stack(new_momentum))
```

```python
import functools
import math

import jax
import jax.numpy as jnp
from jax import lax
from jax.experimental import pallas as pl
from jax.experimental.pallas import tpu as pltpu
from jax.sharding import PartitionSpec as P

ALPHA = 0.9
GAMMA = 0.5
BETA_SCALE = 0.4
CHUNKS = 8
TILE = 512
MESH = pl.DeviceIdType.MESH
BF16 = jnp.bfloat16
F32 = jnp.float32


def loop(n, body):
    def step(i, carry):
        body(i)
        return carry

    lax.fori_loop(0, n, step, 0)


def dot(a, b):
    return jnp.dot(a, b, preferred_element_type=F32)


def kernel(
    beta, width, route, partner, bnd, ctx, w_hbm, m_hbm, so, cg_out, nw_hbm, nm_hbm,
    w, mom, ctx_t, cg, cot, msg, g1, st, g2, part, prec, rrec, bsum, bsend, brecv, fr, sel_b, sel_f, mask,
    ag_s, ag_r, rs_s, rs_r, bk_s, bk_r, fw_s, fw_r, yb_s, yb_r, yf_s, yf_r, cf_s, cf_r, cp_s, cp_r,
    p1_s, p1_r, p2_s, p2_r, w_i, m_i, w_o, m_o,
):
    rep = lax.axis_index("replica")
    sec = lax.axis_index("section")
    ten = lax.axis_index("tensor")
    chip = lax.div(ten, 2)
    core = lax.rem(ten, 2)
    z = lax.div(chip, 2)
    high = lax.rem(chip, 2)
    other = 1 - core
    sibling = (rep, sec, 2 * chip + other)
    right = (lax.rem(rep + 1, 4), sec, ten)
    left = (lax.rem(rep + 3, 4), sec, ten)
    across = (rep, 1 - sec, ten)

    def chip_at(e):
        return lax.rem(z + lax.div(e, 2), 4) * 2 + lax.rem(high + lax.rem(e, 2), 2)

    def rep_at(e):
        return lax.rem(rep + e, 4)

    def peer(e):
        return (rep, sec, 2 * chip_at(e) + core)

    def send(src, dst, ss, rs, to):
        pltpu.make_async_remote_copy(
            src_ref=src, dst_ref=dst, send_sem=ss, recv_sem=rs, device_id=to, device_id_type=MESH
        ).start()

    def sent(ref, sem):
        pltpu.make_async_remote_copy(
            src_ref=ref, dst_ref=ref, send_sem=sem, recv_sem=sem, device_id=sibling, device_id_type=MESH
        ).wait_send()

    def arrived(ref, sem):
        pltpu.make_async_remote_copy(
            src_ref=ref, dst_ref=ref, send_sem=sem, recv_sem=sem, device_id=sibling, device_id_type=MESH
        ).wait_recv()

    def columns(k):
        return pl.ds(pl.multiple_of(k * width, width), width)

    def tiles(body):
        loop(width // TILE, lambda j: body(pl.ds(pl.multiple_of(j * TILE, TILE), TILE)))

    def w_in(k):
        return pltpu.make_async_copy(w_hbm.at[:, columns(k)], w.at[k], w_i.at[k])

    def m_in(k):
        return pltpu.make_async_copy(m_hbm.at[:, columns(k)], mom.at[k], m_i.at[k])

    def w_out(k):
        return pltpu.make_async_copy(w.at[k], nw_hbm.at[:, columns(k)], w_o.at[k])

    def m_out(k):
        return pltpu.make_async_copy(mom.at[k], nm_hbm.at[:, columns(k)], m_o.at[k])

    barrier = pltpu.get_barrier_semaphore()

    def greet(to):
        pl.semaphore_signal(barrier, inc=1, device_id=to, device_id_type=MESH)

    greet(sibling)
    greet(across)
    for e in range(1, 4):
        greet((rep_at(e), sec, ten))
    loop(7, lambda e: greet(peer(e + 1)))
    loop(CHUNKS, lambda k: w_in(k).start())
    loop(CHUNKS, lambda k: m_in(k).start())

    cg[...] = jnp.zeros_like(cg)
    ctx_t[...] = ctx[...].reshape(512, 256).T

    routes = [route[j // 2, j % 2] for j in range(8)]
    slots = []
    for j in range(8):
        before = jnp.int32(0)
        for i in range(j):
            before = before + jnp.where(routes[i] == routes[j], 1, 0)
        slots.append(before)
    count = jnp.int32(0)
    for j in range(8):
        count = count + jnp.where(routes[j] == rep, 1, 0)

    def selector(shape, wide, narrow):
        a = lax.broadcasted_iota(jnp.int32, shape, wide)
        b = lax.broadcasted_iota(jnp.int32, shape, narrow)
        same = jnp.where((a % 16) // 2 == (b % 16) // 2, 1.0, 0.0)
        pair = (a // 16) * 2 + a % 2
        slot = (b // 16) * 2 + b % 2
        total = jnp.zeros(shape, F32)
        for j in range(8):
            mine = jnp.where(routes[j] == rep, 1.0, 0.0).astype(F32)
            total = total + mine * jnp.where((pair == j) & (slot == slots[j]), same, 0.0)
        return total.astype(BF16)

    sel_b[...] = selector((64, 32), 0, 1)
    sel_f[...] = selector((32, 64), 1, 0)
    rows = lax.broadcasted_iota(jnp.int32, (32, 128), 0)
    mask[...] = jnp.where((rows // 16) * 2 + rows % 2 < count, 1.0, 0.0)

    @pl.when(sec == 0)
    def _():
        def clear(k):
            loop(8, lambda c: cot.at[k, core, c, pl.ds(16, 16)].__setitem__(..., jnp.zeros((16, width), BF16)))

        loop(CHUNKS, clear)

    as_one = lambda flag: jnp.where(flag, 1.0, 0.0).astype(F32)
    own_right = as_one(partner[rep_at(1), sec] == rep)
    own_left = as_one(partner[rep_at(3), sec] == rep)
    mine = partner[rep, sec]
    from_left = as_one(mine == rep_at(3))
    from_right = as_one(mine == rep_at(1))
    from_far = as_one(mine == rep_at(2))

    pl.semaphore_wait(barrier, 12)

    def gather(k, count_rows):
        block = cot.at[k, core, chip, pl.ds(0, count_rows)]
        loop(7, lambda e: send(block, block, ag_s.at[k, e], ag_r.at[k, chip], peer(e + 1)))

    def route_back(k):
        cot_rows = bnd[:, columns(k)]
        bsend[k] = dot(sel_b[...], cot_rows).astype(BF16).reshape(4, 16, width)
        for e in (1, 3, 2):
            to = rep_at(e)
            send(bsend.at[k, to], brecv.at[k, rep], bk_s.at[k, e], bk_r.at[k, rep], (to, sec, ten))
        cot[k, core, chip] = (cot_rows.astype(F32) * mask[:, 0:1]).astype(BF16)
        gather(k, 32)

    def cross_back(k):
        total = bsend[k, rep].astype(F32)
        for e in (1, 3, 2):
            source = rep_at(e)
            arrived(brecv.at[k, source], bk_r.at[k, source])
            total = total + brecv[k, source].astype(F32)
        bsend[k, rep] = total.astype(BF16)
        send(bsend.at[k, rep], cot.at[k, core, chip, pl.ds(0, 16)], yb_s.at[k], yb_r.at[k], across)

    def gather_first(k):
        arrived(cot.at[k, core, chip, pl.ds(0, 16)], yb_r.at[k])
        gather(k, 16)

    def share(k):
        def wait_rows(count_rows):
            def one(e):
                source = chip_at(e + 1)
                arrived(cot.at[k, core, source, pl.ds(0, count_rows)], ag_r.at[k, source])

            loop(7, one)

        pl.when(sec == 0)(lambda: wait_rows(16))
        pl.when(sec == 1)(lambda: wait_rows(32))
        send(cot.at[k, core], cot.at[k, core], cf_s.at[k], cf_r.at[k], sibling)

    def cot_tile(k, cols):
        return cot[k, :, :, :, cols].reshape(512, TILE)

    def message(k):
        arrived(cot.at[k, other], cf_r.at[k])
        w_in(k).wait()

        def one(cols):
            grad = dot(ctx_t[...], cot_tile(k, cols))
            out = beta * grad - GAMMA * w[k, :, cols].astype(F32)
            msg[k, :, :, cols] = out.astype(BF16).reshape(2, 128, TILE)

        tiles(one)
        send(msg.at[k, 0], g1.at[k, 0], p1_s.at[k, 0], p1_r.at[k, 0], right)
        send(msg.at[k, 1], g1.at[k, 1], p1_s.at[k, 1], p1_r.at[k, 1], left)

    def context_part(k):
        def one(cols):
            cg[...] += lax.dot_general(
                cot_tile(k, cols), w[k, :, cols], (((1,), (1,)), ((), ())), preferred_element_type=F32
            )

        tiles(one)

    def pass_on(k):
        arrived(g1.at[k, 0], p1_r.at[k, 0])

        def one(cols):
            mixed = own_right * msg[k, 1, :, cols].astype(F32) + (1.0 - own_right) * g1[k, 0, :, cols].astype(F32)
            st[k, 0, :, cols] = mixed.astype(BF16)

        tiles(one)
        send(st.at[k, 0], g2.at[k, 0], p2_s.at[k, 0], p2_r.at[k, 0], right)
        arrived(g1.at[k, 1], p1_r.at[k, 1])

        def two(cols):
            mixed = own_left * msg[k, 0, :, cols].astype(F32) + (1.0 - own_left) * g1[k, 1, :, cols].astype(F32)
            st[k, 1, :, cols] = mixed.astype(BF16)

        tiles(two)
        send(st.at[k, 1], g2.at[k, 1], p2_s.at[k, 1], p2_r.at[k, 1], left)

    def update(k):
        arrived(g2.at[k, 0], p2_r.at[k, 0])
        arrived(g2.at[k, 1], p2_r.at[k, 1])
        m_in(k).wait()

        def one(cols):
            grad = dot(ctx_t[...], cot_tile(k, cols))
            a1, b1 = g1[k, 0, :, cols].astype(F32), g1[k, 1, :, cols].astype(F32)
            a2, b2 = g2[k, 0, :, cols].astype(F32), g2[k, 1, :, cols].astype(F32)
            top = from_left * a1 + from_right * b2 + from_far * a2
            low = from_left * a2 + from_right * b1 + from_far * b2
            for half, theirs in ((0, top), (128, low)):
                at = pl.ds(half, 128)
                current = w[k, at, cols].astype(F32)
                delta = (
                    ALPHA * mom[k, at, cols].astype(F32)
                    - 0.5 * (beta * grad[half : half + 128] + GAMMA * current)
                    - 0.5 * theirs
                )
                mom[k, at, cols] = delta.astype(BF16)
                w[k, at, cols] = (current + delta).astype(BF16)

        tiles(one)
        w_out(k).start()
        m_out(k).start()

    def branch_far(k):
        def one(cols):
            part[k, :, :, cols] = dot(ctx[other], w[k, :, cols]).astype(BF16).reshape(8, 32, TILE)

        tiles(one)
        send(part.at[k], prec.at[k], cp_s.at[k], cp_r.at[k], sibling)

    def branch_near(k):
        arrived(prec.at[k], cp_r.at[k])

        def one(cols):
            own = dot(ctx[core], w[k, :, cols]).reshape(8, 32, TILE)
            prec[k, :, :, cols] = (own + prec[k, :, :, cols].astype(F32)).astype(BF16)

        tiles(one)

        def spread(count_rows):
            def one_peer(e):
                block = prec.at[k, chip_at(e + 1), pl.ds(0, count_rows)]
                to = rrec.at[k, chip, pl.ds(0, count_rows)]
                send(block, to, rs_s.at[k, e], rs_r.at[k, chip], peer(e + 1))

            loop(7, one_peer)

        pl.when(sec == 0)(lambda: spread(16))
        pl.when(sec == 1)(lambda: spread(32))

    def reduce_rows(k, count_rows):
        at = pl.ds(0, count_rows)

        def wait_one(e):
            source = chip_at(e + 1)
            arrived(rrec.at[k, source, at], rs_r.at[k, source])

        loop(7, wait_one)
        total = prec[k, chip, at].astype(F32)
        for e in range(1, 8):
            total = total + rrec[k, chip_at(e), at].astype(F32)
        return total

    def reduce_first(k):
        total = reduce_rows(k, 16)
        stream = (bnd[pl.ds(0, 16), columns(k)].astype(F32) + total).astype(BF16)
        so[pl.ds(0, 16), columns(k)] = stream
        so[pl.ds(16, 16), columns(k)] = jnp.zeros_like(stream)
        fr[k, rep] = stream
        send(fr.at[k, rep], fr.at[k, rep], yf_s.at[k], yf_r.at[k], across)

    def reduce_second(k):
        bsum[k] = reduce_rows(k, 32)

    def route_ahead(k):
        arrived(fr.at[k, rep], yf_r.at[k])
        for e in (1, 3, 2):
            to = rep_at(e)
            send(fr.at[k, rep], fr.at[k, rep], fw_s.at[k, e], fw_r.at[k, rep], (to, sec, ten))

    def finish_second(k):
        for e in (1, 3, 2):
            source = rep_at(e)
            arrived(fr.at[k, source], fw_r.at[k, source])
        total = dot(sel_f[...], fr[k].reshape(64, width)) + bsum[k]
        so[:, columns(k)] = (total.astype(BF16).astype(F32) * mask[:, 0:1]).astype(BF16)

    late = 1 - sec
    stages = (
        (0, 1, route_back),
        (1, 1, cross_back),
        (2, 0, gather_first),
        (2 + late, None, share),
        (3 + late, None, message),
        (4 + late, None, pass_on),
        (3 + late, None, context_part),
        (3 + late, None, branch_far),
        (4 + late, None, branch_near),
        (5 + late, None, update),
        (5 + late, 0, reduce_first),
        (5 + late, 1, reduce_second),
        (6, 1, route_ahead),
        (7, 1, finish_second),
    )

    def step(i):
        for lag, only, stage in stages:
            k = i - lag
            live = (k >= 0) & (k < CHUNKS)
            if only is not None:
                live = live & (sec == only)
            pl.when(live)(functools.partial(stage, k))

    loop(CHUNKS + 7, step)

    cg_out[...] = cg[...].astype(BF16)

    def drain(k):
        def rows_sent(count_rows):
            def one(e):
                sent(cot.at[k, core, chip, pl.ds(0, count_rows)], ag_s.at[k, e])
                sent(prec.at[k, chip, pl.ds(0, count_rows)], rs_s.at[k, e])

            loop(7, one)

        @pl.when(sec == 0)
        def _():
            rows_sent(16)
            sent(fr.at[k, rep], yf_s.at[k])

        @pl.when(sec == 1)
        def _():
            rows_sent(32)
            sent(bsend.at[k, rep], yb_s.at[k])
            for e in (1, 2, 3):
                sent(bsend.at[k, rep], bk_s.at[k, e])
                sent(fr.at[k, rep], fw_s.at[k, e])

        sent(cot.at[k, core], cf_s.at[k])
        sent(part.at[k], cp_s.at[k])
        for half in (0, 1):
            sent(msg.at[k, half], p1_s.at[k, half])
            sent(st.at[k, half], p2_s.at[k, half])
        w_out(k).wait()
        m_out(k).wait()

    loop(CHUNKS, drain)


def local(boundary, context, weights, momentum, route, partner):
    beta = BETA_SCALE / math.sqrt(512)
    model = weights.shape[-1]
    width = model // CHUNKS
    bnd = boundary.reshape(8, 2, 2, model).transpose(1, 0, 2, 3).reshape(32, model)
    ctx = context.reshape(8, 2, 8, 2, 2, 256).transpose(1, 0, 3, 2, 4, 5).reshape(2, 256, 256)
    n = CHUNKS
    dma = pltpu.SemaphoreType.DMA
    scratch = [
        pltpu.VMEM((n, 256, width), BF16),
        pltpu.VMEM((n, 256, width), BF16),
        pltpu.VMEM((256, 512), BF16),
        pltpu.VMEM((512, 256), F32),
        pltpu.VMEM((n, 2, 8, 32, width), BF16),
        pltpu.VMEM((n, 2, 128, width), BF16),
        pltpu.VMEM((n, 2, 128, width), BF16),
        pltpu.VMEM((n, 2, 128, width), BF16),
        pltpu.VMEM((n, 2, 128, width), BF16),
        pltpu.VMEM((n, 8, 32, width), BF16),
        pltpu.VMEM((n, 8, 32, width), BF16),
        pltpu.VMEM((n, 8, 32, width), BF16),
        pltpu.VMEM((n, 32, width), F32),
        pltpu.VMEM((n, 4, 16, width), BF16),
        pltpu.VMEM((n, 4, 16, width), BF16),
        pltpu.VMEM((n, 4, 16, width), BF16),
        pltpu.VMEM((64, 32), BF16),
        pltpu.VMEM((32, 64), BF16),
        pltpu.VMEM((32, 128), F32),
        *[dma((n, 8))] * 4,
        *[dma((n, 4))] * 4,
        *[dma((n,))] * 8,
        *[dma((n, 2))] * 4,
        *[dma((n,))] * 4,
    ]
    vmem = pl.BlockSpec(memory_space=pltpu.VMEM)
    smem = pl.BlockSpec(memory_space=pltpu.SMEM)
    anywhere = pl.BlockSpec(memory_space=pl.ANY)
    stream, ctx_grad, new_weights, new_momentum = pl.pallas_call(
        functools.partial(kernel, beta, width),
        out_shape=(
            jax.ShapeDtypeStruct((32, model), BF16),
            jax.ShapeDtypeStruct((512, 256), BF16),
            jax.ShapeDtypeStruct((256, model), BF16),
            jax.ShapeDtypeStruct((256, model), BF16),
        ),
        in_specs=[smem, smem, vmem, vmem, anywhere, anywhere],
        out_specs=(vmem, vmem, anywhere, anywhere),
        scratch_shapes=scratch,
        compiler_params=pltpu.CompilerParams(
            collective_id=0, has_side_effects=True, vmem_limit_bytes=62 * 2**20
        ),
        name="noloco_step",
    )(route, partner, bnd, ctx, weights[0, 0], momentum[0, 0])
    stream = stream.reshape(2, 8, 2, model).transpose(1, 0, 2, 3).reshape(1, 1, 8, 4, model)
    ctx_grad = ctx_grad.reshape(2, 8, 2, 8, 2, 256).transpose(1, 0, 3, 2, 4, 5).reshape(1, 1, 128, 4, 256)
    return stream, ctx_grad, new_weights[None, None], new_momentum[None, None]


def solution(mesh):
    in_specs = (
        P("replica", "section", "tensor", None, None),
        P("replica", "section", None, None, "tensor"),
        P("replica", "section", "tensor", None),
        P("replica", "section", "tensor", None),
        P(),
        P(),
    )
    out_specs = (
        P("replica", "section", "tensor", None, None),
        P("replica", "section", None, None, "tensor"),
        P("replica", "section", "tensor", None),
        P("replica", "section", "tensor", None),
    )
    return jax.shard_map(local, mesh=mesh, in_specs=in_specs, out_specs=out_specs, check_vma=False)
```

```python
import functools
import math

import jax
import jax.numpy as jnp
from jax import lax
from jax.experimental import pallas as pl
from jax.experimental.pallas import tpu as pltpu
from jax.sharding import PartitionSpec as P

ALPHA = 0.9
GAMMA = 0.5
BETA_SCALE = 0.4
CHUNKS = 8
AHEAD = 8
TILE = 512
MESH = pl.DeviceIdType.MESH
BF16 = jnp.bfloat16
F32 = jnp.float32


def loop(n, body):
    def step(i, carry):
        body(i)
        return carry

    lax.fori_loop(0, n, step, 0)


def dot(a, b):
    return jnp.dot(a, b, preferred_element_type=F32)


def kernel(
    beta, width, route, partner, bnd, ctx, w_hbm, m_hbm, so, cg_out, w, mom,
    ctx_t, cg, cot, msg, g1, st, g2, part, prec, rrec, bsum, bsend, brecv, fr, yb, sel_b, sel_f, mask,
    ag_s, ag_r, rs_s, rs_r, bk_s, bk_r, fw_s, fw_r, yb_s, yb_r, yf_s, yf_r, cf_s, cf_r, cp_s, cp_r,
    p1_s, p1_r, p2_s, p2_r, w_i, m_i,
):
    rep = lax.axis_index("replica")
    sec = lax.axis_index("section")
    ten = lax.axis_index("tensor")
    chip = lax.div(ten, 2)
    core = lax.rem(ten, 2)
    z = lax.div(chip, 2)
    high = lax.rem(chip, 2)
    other = 1 - core
    sibling = (rep, sec, 2 * chip + other)
    right = (lax.rem(rep + 1, 4), sec, ten)
    left = (lax.rem(rep + 3, 4), sec, ten)
    across = (rep, 1 - sec, ten)

    def chip_at(e):
        return lax.rem(z + lax.div(e, 2), 4) * 2 + lax.rem(high + lax.rem(e, 2), 2)

    def rep_at(e):
        return lax.rem(rep + e, 4)

    def peer(e):
        return (rep, sec, 2 * chip_at(e) + core)

    def send(src, dst, ss, rs, to):
        pltpu.make_async_remote_copy(
            src_ref=src, dst_ref=dst, send_sem=ss, recv_sem=rs, device_id=to, device_id_type=MESH
        ).start()

    def sent(ref, sem):
        pltpu.make_async_remote_copy(
            src_ref=ref, dst_ref=ref, send_sem=sem, recv_sem=sem, device_id=sibling, device_id_type=MESH
        ).wait_send()

    def arrived(ref, sem):
        pltpu.make_async_remote_copy(
            src_ref=ref, dst_ref=ref, send_sem=sem, recv_sem=sem, device_id=sibling, device_id_type=MESH
        ).wait_recv()

    def columns(k):
        return pl.ds(pl.multiple_of(k * width, width), width)

    def tiles(body):
        loop(width // TILE, lambda j: body(pl.ds(pl.multiple_of(j * TILE, TILE), TILE)))

    def model(k, body):
        def one(j):
            whole = pl.multiple_of(k * width + j * TILE, TILE)
            body(pl.ds(pl.multiple_of(j * TILE, TILE), TILE), pl.ds(whole, TILE))

        loop(width // TILE, one)

    def w_in(k):
        return pltpu.make_async_copy(w_hbm.at[:, columns(k)], w.at[:, columns(k)], w_i.at[k])

    def m_in(k):
        return pltpu.make_async_copy(m_hbm.at[:, columns(k)], mom.at[:, columns(k)], m_i.at[k])

    barrier = pltpu.get_barrier_semaphore()

    def greet(to):
        pl.semaphore_signal(barrier, inc=1, device_id=to, device_id_type=MESH)

    greet(sibling)
    greet(across)
    for e in range(1, 4):
        greet((rep_at(e), sec, ten))
    loop(7, lambda e: greet(peer(e + 1)))
    loop(CHUNKS, lambda k: w_in(k).start())
    loop(CHUNKS, lambda k: m_in(k).start())

    routes = [route[j % 2, j // 2] for j in range(8)]
    slots = []
    for j in range(8):
        before = jnp.int32(0)
        for i in range(j):
            before = before + jnp.where(routes[i] == routes[j], 1, 0)
        slots.append(before)
    count = jnp.int32(0)
    for j in range(8):
        count = count + jnp.where(routes[j] == rep, 1, 0)

    def selector(shape, wide, narrow):
        a = lax.broadcasted_iota(jnp.int32, shape, wide)
        b = lax.broadcasted_iota(jnp.int32, shape, narrow)
        same = jnp.where(a % 8 == b % 8, 1.0, 0.0)
        pair, slot = a // 8, b // 8
        total = jnp.zeros(shape, F32)
        for j in range(8):
            mine = jnp.where(routes[j] == rep, 1.0, 0.0).astype(F32)
            total = total + mine * jnp.where((pair == j) & (slot == slots[j]), same, 0.0)
        return total.astype(BF16)

    sel_b[...] = selector((64, 32), 0, 1)
    rows = lax.broadcasted_iota(jnp.int32, (32, 128), 0)
    mask[...] = jnp.where(rows // 8 < count, 1.0, 0.0)

    as_one = lambda flag: jnp.where(flag, 1.0, 0.0).astype(F32)
    own_right = as_one(partner[sec, rep_at(1)] == rep)
    own_left = as_one(partner[sec, rep_at(3)] == rep)
    mine = partner[sec, rep]
    from_left = as_one(mine == rep_at(3))
    from_right = as_one(mine == rep_at(1))
    from_far = as_one(mine == rep_at(2))

    pl.semaphore_wait(barrier, 12)

    def gather(k, count_rows):
        block = cot.at[k, core, chip, pl.ds(0, count_rows)]
        loop(7, lambda e: send(block, block, ag_s.at[k, e], ag_r.at[k, chip], peer(e + 1)))

    def route_back(k):
        bsend[k] = dot(sel_b[...], bnd[:, columns(k)]).astype(BF16).reshape(4, 16, width)
        for e in (1, 3, 2):
            to = rep_at(e)
            send(bsend.at[k, to], brecv.at[k, rep], bk_s.at[k, e], bk_r.at[k, rep], (to, sec, ten))

    def cross_back(k):
        total = bsend[k, rep].astype(F32)
        for e in (1, 3, 2):
            source = rep_at(e)
            arrived(brecv.at[k, source], bk_r.at[k, source])
            total = total + brecv[k, source].astype(F32)
        yb[k] = total.astype(BF16)
        send(yb.at[k], cot.at[k, core, chip, pl.ds(0, 16)], yb_s.at[k], yb_r.at[k], across)

    def gather_first(k):
        arrived(cot.at[k, core, chip, pl.ds(0, 16)], yb_r.at[k])
        gather(k, 16)

    def gather_second(k):
        cot[k, core, chip] = (bnd[:, columns(k)].astype(F32) * mask[:, 0:1]).astype(BF16)
        gather(k, 32)

    def share(k):
        def wait_rows(count_rows):
            def one(e):
                source = chip_at(e + 1)
                arrived(cot.at[k, core, source, pl.ds(0, count_rows)], ag_r.at[k, source])

            loop(7, one)

        pl.when(sec == 0)(lambda: wait_rows(16))
        pl.when(sec == 1)(lambda: wait_rows(32))
        send(cot.at[k, core], cot.at[k, core], cf_s.at[k], cf_r.at[k], sibling)

    def cot_tile(k, cols):
        return cot[k, :, :, :, cols].reshape(512, TILE)

    def message(k):
        arrived(cot.at[k, other], cf_r.at[k])

        def one(cols, whole):
            grad = dot(ctx_t[...], cot_tile(k, cols))
            out = beta * grad - GAMMA * w[:, whole].astype(F32)
            msg[k, :, :, cols] = out.astype(BF16).reshape(2, 128, TILE)

        model(k, one)
        send(msg.at[k, 0], g1.at[k, 0], p1_s.at[k, 0], p1_r.at[k, 0], right)
        send(msg.at[k, 1], g1.at[k, 1], p1_s.at[k, 1], p1_r.at[k, 1], left)

    def context_part(k):
        def one(cols, whole):
            cg[...] += lax.dot_general(
                cot_tile(k, cols), w[:, whole], (((1,), (1,)), ((), ())), preferred_element_type=F32
            )

        model(k, one)

    def pass_on(k):
        arrived(g1.at[k, 0], p1_r.at[k, 0])

        def one(cols):
            mixed = own_right * msg[k, 1, :, cols].astype(F32) + (1.0 - own_right) * g1[k, 0, :, cols].astype(F32)
            st[k, 0, :, cols] = mixed.astype(BF16)

        tiles(one)
        send(st.at[k, 0], g2.at[k, 0], p2_s.at[k, 0], p2_r.at[k, 0], right)
        arrived(g1.at[k, 1], p1_r.at[k, 1])

        def two(cols):
            mixed = own_left * msg[k, 0, :, cols].astype(F32) + (1.0 - own_left) * g1[k, 1, :, cols].astype(F32)
            st[k, 1, :, cols] = mixed.astype(BF16)

        tiles(two)
        send(st.at[k, 1], g2.at[k, 1], p2_s.at[k, 1], p2_r.at[k, 1], left)

    def update(k):
        arrived(g2.at[k, 0], p2_r.at[k, 0])
        arrived(g2.at[k, 1], p2_r.at[k, 1])
        m_in(k).wait()

        def one(cols, whole):
            grad = dot(ctx_t[...], cot_tile(k, cols))
            a1, b1 = g1[k, 0, :, cols].astype(F32), g1[k, 1, :, cols].astype(F32)
            a2, b2 = g2[k, 0, :, cols].astype(F32), g2[k, 1, :, cols].astype(F32)
            top = from_left * a1 + from_right * b2 + from_far * a2
            low = from_left * a2 + from_right * b1 + from_far * b2
            for half, theirs in ((0, top), (128, low)):
                at = pl.ds(half, 128)
                current = w[at, whole].astype(F32)
                delta = (
                    ALPHA * mom[at, whole].astype(F32)
                    - 0.5 * (beta * grad[half : half + 128] + GAMMA * current)
                    - 0.5 * theirs
                )
                mom[at, whole] = delta.astype(BF16)
                w[at, whole] = (current + delta).astype(BF16)

        model(k, one)

    def branch_far(k):
        def one(cols, whole):
            part[k, :, :, cols] = dot(ctx[other], w[:, whole]).astype(BF16).reshape(8, 32, TILE)

        model(k, one)
        send(part.at[k], prec.at[k], cp_s.at[k], cp_r.at[k], sibling)

    def branch_near(k):
        arrived(prec.at[k], cp_r.at[k])

        def one(cols, whole):
            own = dot(ctx[core], w[:, whole]).reshape(8, 32, TILE)
            prec[k, :, :, cols] = (own + prec[k, :, :, cols].astype(F32)).astype(BF16)

        model(k, one)

        def spread(count_rows):
            def one_peer(e):
                block = prec.at[k, chip_at(e + 1), pl.ds(0, count_rows)]
                to = rrec.at[k, chip, pl.ds(0, count_rows)]
                send(block, to, rs_s.at[k, e], rs_r.at[k, chip], peer(e + 1))

            loop(7, one_peer)

        pl.when(sec == 0)(lambda: spread(16))
        pl.when(sec == 1)(lambda: spread(32))

    def reduce_rows(k, count_rows):
        at = pl.ds(0, count_rows)

        def wait_one(e):
            source = chip_at(e + 1)
            arrived(rrec.at[k, source, at], rs_r.at[k, source])

        loop(7, wait_one)
        total = prec[k, chip, at].astype(F32)
        for e in range(1, 8):
            total = total + rrec[k, chip_at(e), at].astype(F32)
        return total

    def reduce_first(k):
        total = reduce_rows(k, 16)
        stream = (bnd[pl.ds(0, 16), columns(k)].astype(F32) + total).astype(BF16)
        so[pl.ds(0, 16), columns(k)] = stream
        so[pl.ds(16, 16), columns(k)] = jnp.zeros_like(stream)
        fr[k, rep] = stream
        send(fr.at[k, rep], fr.at[k, rep], yf_s.at[k], yf_r.at[k], across)

    def reduce_second(k):
        bsum[k] = reduce_rows(k, 32)

    def route_ahead(k):
        arrived(fr.at[k, rep], yf_r.at[k])
        for e in (1, 3, 2):
            to = rep_at(e)
            send(fr.at[k, rep], fr.at[k, rep], fw_s.at[k, e], fw_r.at[k, rep], (to, sec, ten))

    def finish_second(k):
        for e in (1, 3, 2):
            source = rep_at(e)
            arrived(fr.at[k, source], fw_r.at[k, source])
        total = dot(sel_f[...], fr[k].reshape(64, width)) + bsum[k]
        so[:, columns(k)] = (total.astype(BF16).astype(F32) * mask[:, 0:1]).astype(BF16)

    @pl.when(sec == 1)
    def _():
        route_back(0)
        gather_second(0)
        loop(CHUNKS - 1, lambda k: route_back(k + 1))

    cg[...] = jnp.zeros_like(cg)
    ctx_t[...] = ctx[...].reshape(512, 256).T
    sel_f[...] = selector((32, 64), 1, 0)

    @pl.when(sec == 0)
    def _():
        def clear(k):
            loop(8, lambda c: cot.at[k, core, c, pl.ds(16, 16)].__setitem__(..., jnp.zeros((16, width), BF16)))

        loop(CHUNKS, clear)

    late = 1 - sec
    stages = (
        (2, None, lambda k: w_in(k).wait()),
        (2 + late, None, message),
        (4 + late, None, pass_on),
        (1, 0, gather_first),
        (None, 1, cross_back),
        (-1, 1, gather_second),
        (1 + late, None, share),
        (2, None, branch_far),
        (4, None, branch_near),
        (6, 0, reduce_first),
        (6, 1, reduce_second),
        (AHEAD, 1, route_ahead),
        (AHEAD + 2, 1, finish_second),
        (2 + late, None, context_part),
        (6 + late, None, update),
    )

    def run(live, only, stage, k):
        live = live & (k < CHUNKS)
        if only is not None:
            live = live & (sec == only)
        pl.when(live)(functools.partial(stage, k))

    def step(i):
        for lag, only, stage in stages:
            if lag is None:
                run(i >= 1, only, stage, 2 * i - 1)
                run(i >= 0, only, stage, 2 * i)
            else:
                k = i - lag
                run((k >= 0) & (i >= 0), only, stage, k)

    loop(CHUNKS + AHEAD + 2, step)

    cg_out[...] = cg[...].astype(BF16)

    def drain(k):
        def rows_sent(count_rows):
            def one(e):
                sent(cot.at[k, core, chip, pl.ds(0, count_rows)], ag_s.at[k, e])
                sent(prec.at[k, chip, pl.ds(0, count_rows)], rs_s.at[k, e])

            loop(7, one)

        @pl.when(sec == 0)
        def _():
            rows_sent(16)
            sent(fr.at[k, rep], yf_s.at[k])

        @pl.when(sec == 1)
        def _():
            rows_sent(32)
            sent(yb.at[k], yb_s.at[k])
            for e in (1, 2, 3):
                sent(bsend.at[k, rep], bk_s.at[k, e])
                sent(fr.at[k, rep], fw_s.at[k, e])

        sent(cot.at[k, core], cf_s.at[k])
        sent(part.at[k], cp_s.at[k])
        for half in (0, 1):
            sent(msg.at[k, half], p1_s.at[k, half])
            sent(st.at[k, half], p2_s.at[k, half])

    loop(CHUNKS, drain)


def local(boundary, context, weights, momentum, route, partner):
    beta = BETA_SCALE / math.sqrt(512)
    model = weights.shape[-1]
    width = model // CHUNKS
    bnd = boundary.reshape(8, 4, model).transpose(1, 0, 2).reshape(32, model)
    ctx = context.reshape(8, 2, 8, 4, 256).transpose(1, 0, 3, 2, 4).reshape(2, 256, 256)
    n = CHUNKS
    dma = pltpu.SemaphoreType.DMA
    scratch = [
        pltpu.VMEM((256, 512), BF16),
        pltpu.VMEM((512, 256), F32),
        pltpu.VMEM((n, 2, 8, 32, width), BF16),
        pltpu.VMEM((n, 2, 128, width), BF16),
        pltpu.VMEM((n, 2, 128, width), BF16),
        pltpu.VMEM((n, 2, 128, width), BF16),
        pltpu.VMEM((n, 2, 128, width), BF16),
        pltpu.VMEM((n, 8, 32, width), BF16),
        pltpu.VMEM((n, 8, 32, width), BF16),
        pltpu.VMEM((n, 8, 32, width), BF16),
        pltpu.VMEM((n, 32, width), F32),
        pltpu.VMEM((n, 4, 16, width), BF16),
        pltpu.VMEM((n, 4, 16, width), BF16),
        pltpu.VMEM((n, 4, 16, width), BF16),
        pltpu.VMEM((n, 16, width), BF16),
        pltpu.VMEM((64, 32), BF16),
        pltpu.VMEM((32, 64), BF16),
        pltpu.VMEM((32, 128), F32),
        *[dma((n, 8))] * 4,
        *[dma((n, 4))] * 4,
        *[dma((n,))] * 8,
        *[dma((n, 2))] * 4,
        *[dma((n,))] * 2,
    ]
    vmem = pl.BlockSpec(memory_space=pltpu.VMEM)
    smem = pl.BlockSpec(memory_space=pltpu.SMEM)
    anywhere = pl.BlockSpec(memory_space=pl.ANY)
    stream, ctx_grad, new_weights, new_momentum = pl.pallas_call(
        functools.partial(kernel, beta, width),
        out_shape=(
            pltpu.VMEM((32, model), BF16),
            pltpu.VMEM((512, 256), BF16),
            pltpu.VMEM((256, model), BF16),
            pltpu.VMEM((256, model), BF16),
        ),
        in_specs=[smem, smem, vmem, vmem, anywhere, anywhere],
        out_specs=(vmem, vmem, vmem, vmem),
        scratch_shapes=scratch,
        compiler_params=pltpu.CompilerParams(
            collective_id=0, has_side_effects=True, vmem_limit_bytes=48 * 2**20
        ),
        name="noloco_step",
    )(route.T, partner.T, bnd, ctx, weights[0, 0], momentum[0, 0])
    stream = stream.reshape(4, 8, model).transpose(1, 0, 2).reshape(1, 1, 8, 4, model)
    ctx_grad = ctx_grad.reshape(2, 8, 4, 8, 256).transpose(1, 0, 3, 2, 4).reshape(1, 1, 128, 4, 256)
    return stream, ctx_grad, new_weights[None, None], new_momentum[None, None]


def solution(mesh):
    in_specs = (
        P("replica", "section", "tensor", None, None),
        P("replica", "section", None, None, "tensor"),
        P("replica", "section", "tensor", None),
        P("replica", "section", "tensor", None),
        P(),
        P(),
    )
    out_specs = (
        P("replica", "section", "tensor", None, None),
        P("replica", "section", None, None, "tensor"),
        P("replica", "section", "tensor", None),
        P("replica", "section", "tensor", None),
    )
    return jax.shard_map(local, mesh=mesh, in_specs=in_specs, out_specs=out_specs, check_vma=False)
```

```python
import functools
import math

import jax
import jax.numpy as jnp
from jax import lax
from jax.experimental import pallas as pl
from jax.experimental.pallas import tpu as pltpu
from jax.sharding import PartitionSpec as P

ALPHA = 0.9
GAMMA = 0.5
BETA_SCALE = 0.4
CHUNKS = 16
AHEAD = 8
TILE = 512
MESH = pl.DeviceIdType.MESH
BF16 = jnp.bfloat16
F32 = jnp.float32


def loop(n, body):
    def step(i, carry):
        body(i)
        return carry

    lax.fori_loop(0, n, step, 0)


def dot(a, b):
    return jnp.dot(a, b, preferred_element_type=F32)


def kernel(
    beta, width, route, partner, bnd, ctx, w_hbm, m_hbm, so, cg_out, w, mom,
    ctx_t, cg, cot, msg, g1, st, g2, part, prec, rrec, bsum, bsend, brecv, fr, yb, sel_b, sel_f, mask,
    ag_s, ag_r, rs_s, rs_r, bk_s, bk_r, fw_s, fw_r, yb_s, yb_r, yf_s, yf_r, cf_s, cf_r, cp_s, cp_r,
    p1_s, p1_r, p2_s, p2_r, w_i, m_i,
):
    rep = lax.axis_index("replica")
    sec = lax.axis_index("section")
    ten = lax.axis_index("tensor")
    chip = lax.div(ten, 2)
    core = lax.rem(ten, 2)
    z = lax.div(chip, 2)
    high = lax.rem(chip, 2)
    other = 1 - core
    sibling = (rep, sec, 2 * chip + other)
    right = (lax.rem(rep + 1, 4), sec, ten)
    left = (lax.rem(rep + 3, 4), sec, ten)
    across = (rep, 1 - sec, ten)

    def chip_at(e):
        return lax.rem(z + lax.div(e, 2), 4) * 2 + lax.rem(high + lax.rem(e, 2), 2)

    def rep_at(e):
        return lax.rem(rep + e, 4)

    def peer(e):
        return (rep, sec, 2 * chip_at(e) + core)

    def send(src, dst, ss, rs, to):
        pltpu.make_async_remote_copy(
            src_ref=src, dst_ref=dst, send_sem=ss, recv_sem=rs, device_id=to, device_id_type=MESH
        ).start()

    def sent(ref, sem):
        pltpu.make_async_remote_copy(
            src_ref=ref, dst_ref=ref, send_sem=sem, recv_sem=sem, device_id=sibling, device_id_type=MESH
        ).wait_send()

    def arrived(ref, sem):
        pltpu.make_async_remote_copy(
            src_ref=ref, dst_ref=ref, send_sem=sem, recv_sem=sem, device_id=sibling, device_id_type=MESH
        ).wait_recv()

    def seven(ref, count_rows):
        return ref.at[pl.ds(0, 7), pl.ds(0, count_rows)]

    def columns(k):
        return pl.ds(pl.multiple_of(k * width, width), width)

    def tiles(body):
        loop(width // TILE, lambda j: body(pl.ds(pl.multiple_of(j * TILE, TILE), TILE)))

    def model(k, body):
        def one(j):
            whole = pl.multiple_of(k * width + j * TILE, TILE)
            body(pl.ds(pl.multiple_of(j * TILE, TILE), TILE), pl.ds(whole, TILE))

        loop(width // TILE, one)

    def w_in(k):
        return pltpu.make_async_copy(w_hbm.at[:, columns(k)], w.at[:, columns(k)], w_i.at[k])

    def m_in(k):
        return pltpu.make_async_copy(m_hbm.at[:, columns(k)], mom.at[:, columns(k)], m_i.at[k])

    barrier = pltpu.get_barrier_semaphore()

    def greet(to):
        pl.semaphore_signal(barrier, inc=1, device_id=to, device_id_type=MESH)

    greet(sibling)
    greet(across)
    for e in range(1, 4):
        greet((rep_at(e), sec, ten))
    loop(7, lambda e: greet(peer(e + 1)))
    loop(CHUNKS, lambda k: w_in(k).start())
    loop(CHUNKS, lambda k: m_in(k).start())

    routes = [route[j % 2, j // 2] for j in range(8)]
    slots = []
    for j in range(8):
        before = jnp.int32(0)
        for i in range(j):
            before = before + jnp.where(routes[i] == routes[j], 1, 0)
        slots.append(before)
    count = jnp.int32(0)
    for j in range(8):
        count = count + jnp.where(routes[j] == rep, 1, 0)

    def selector(shape, wide, narrow):
        a = lax.broadcasted_iota(jnp.int32, shape, wide)
        b = lax.broadcasted_iota(jnp.int32, shape, narrow)
        same = jnp.where(a % 8 == b % 8, 1.0, 0.0)
        pair, slot = a // 8, b // 8
        total = jnp.zeros(shape, F32)
        for j in range(8):
            mine = jnp.where(routes[j] == rep, 1.0, 0.0).astype(F32)
            total = total + mine * jnp.where((pair == j) & (slot == slots[j]), same, 0.0)
        return total.astype(BF16)

    sel_b[...] = selector((64, 32), 0, 1)
    rows = lax.broadcasted_iota(jnp.int32, (32, 128), 0)
    mask[...] = jnp.where(rows // 8 < count, 1.0, 0.0)

    as_one = lambda flag: jnp.where(flag, 1.0, 0.0).astype(F32)
    own_right = as_one(partner[sec, rep_at(1)] == rep)
    own_left = as_one(partner[sec, rep_at(3)] == rep)
    mine = partner[sec, rep]
    from_left = as_one(mine == rep_at(3))
    from_right = as_one(mine == rep_at(1))
    from_far = as_one(mine == rep_at(2))

    pl.semaphore_wait(barrier, 12)

    def gather(k, count_rows):
        block = cot.at[k, core, chip, pl.ds(0, count_rows)]
        loop(7, lambda e: send(block, block, ag_s.at[k], ag_r.at[k], peer(e + 1)))

    def route_back(k):
        bsend[k] = dot(sel_b[...], bnd[:, columns(k)]).astype(BF16).reshape(4, 16, width)
        for e in (1, 3, 2):
            to = rep_at(e)
            send(bsend.at[k, to], brecv.at[k, rep], bk_s.at[k], bk_r.at[k], (to, sec, ten))

    def cross_back(k):
        total = bsend[k, rep].astype(F32)
        arrived(brecv.at[k, pl.ds(0, 3)], bk_r.at[k])
        for e in (1, 3, 2):
            total = total + brecv[k, rep_at(e)].astype(F32)
        yb[k, 0] = total.astype(BF16)
        send(yb.at[k, 0], cot.at[k, core, chip, pl.ds(0, 16)], yb_s.at[k], yb_r.at[k], across)

    def gather_first(k):
        arrived(cot.at[k, core, chip, pl.ds(0, 16)], yb_r.at[k])
        gather(k, 16)

    def gather_second(k):
        cot[k, core, chip] = (bnd[:, columns(k)].astype(F32) * mask[:, 0:1]).astype(BF16)
        gather(k, 32)

    def share(k):
        pl.when(sec == 0)(lambda: arrived(seven(cot.at[k, core], 16), ag_r.at[k]))
        pl.when(sec == 1)(lambda: arrived(seven(cot.at[k, core], 32), ag_r.at[k]))
        send(cot.at[k, core], cot.at[k, core], cf_s.at[k], cf_r.at[k], sibling)

    def cot_tile(k, cols):
        return cot[k, :, :, :, cols].reshape(512, TILE)

    def message(k):
        arrived(cot.at[k, other], cf_r.at[k])

        def one(cols, whole):
            grad = dot(ctx_t[...], cot_tile(k, cols))
            out = beta * grad - GAMMA * w[:, whole].astype(F32)
            msg[k, :, :, cols] = out.astype(BF16).reshape(2, 128, TILE)

        model(k, one)
        send(msg.at[k, 0], g1.at[k, 0], p1_s.at[k], p1_r.at[k, 0], right)
        send(msg.at[k, 1], g1.at[k, 1], p1_s.at[k], p1_r.at[k, 1], left)

    def context_part(k):
        def one(cols, whole):
            cg[...] += lax.dot_general(
                cot_tile(k, cols), w[:, whole], (((1,), (1,)), ((), ())), preferred_element_type=F32
            )

        model(k, one)

    def pass_on(k):
        arrived(g1.at[k, 0], p1_r.at[k, 0])

        def one(cols):
            mixed = own_right * msg[k, 1, :, cols].astype(F32) + (1.0 - own_right) * g1[k, 0, :, cols].astype(F32)
            st[k, 0, :, cols] = mixed.astype(BF16)

        tiles(one)
        send(st.at[k, 0], g2.at[k, 0], p2_s.at[k], p2_r.at[k], right)
        arrived(g1.at[k, 1], p1_r.at[k, 1])

        def two(cols):
            mixed = own_left * msg[k, 0, :, cols].astype(F32) + (1.0 - own_left) * g1[k, 1, :, cols].astype(F32)
            st[k, 1, :, cols] = mixed.astype(BF16)

        tiles(two)
        send(st.at[k, 1], g2.at[k, 1], p2_s.at[k], p2_r.at[k], left)

    def update(k):
        arrived(g2.at[k], p2_r.at[k])
        m_in(k).wait()

        def one(cols, whole):
            grad = dot(ctx_t[...], cot_tile(k, cols))
            a1, b1 = g1[k, 0, :, cols].astype(F32), g1[k, 1, :, cols].astype(F32)
            a2, b2 = g2[k, 0, :, cols].astype(F32), g2[k, 1, :, cols].astype(F32)
            top = from_left * a1 + from_right * b2 + from_far * a2
            low = from_left * a2 + from_right * b1 + from_far * b2
            for half, theirs in ((0, top), (128, low)):
                at = pl.ds(half, 128)
                current = w[at, whole].astype(F32)
                delta = (
                    ALPHA * mom[at, whole].astype(F32)
                    - 0.5 * (beta * grad[half : half + 128] + GAMMA * current)
                    - 0.5 * theirs
                )
                mom[at, whole] = delta.astype(BF16)
                w[at, whole] = (current + delta).astype(BF16)

        model(k, one)

    def branch_far(k):
        def one(cols, whole):
            part[k, :, :, cols] = dot(ctx[other], w[:, whole]).astype(BF16).reshape(8, 32, TILE)

        model(k, one)
        send(part.at[k], prec.at[k], cp_s.at[k], cp_r.at[k], sibling)

    def branch_near(k):
        arrived(prec.at[k], cp_r.at[k])

        def one(cols, whole):
            own = dot(ctx[core], w[:, whole]).reshape(8, 32, TILE)
            prec[k, :, :, cols] = (own + prec[k, :, :, cols].astype(F32)).astype(BF16)

        model(k, one)

        def spread(count_rows):
            def one_peer(e):
                block = prec.at[k, chip_at(e + 1), pl.ds(0, count_rows)]
                to = rrec.at[k, chip, pl.ds(0, count_rows)]
                send(block, to, rs_s.at[k], rs_r.at[k], peer(e + 1))

            loop(7, one_peer)

        pl.when(sec == 0)(lambda: spread(16))
        pl.when(sec == 1)(lambda: spread(32))

    def reduce_rows(k, count_rows):
        at = pl.ds(0, count_rows)

        arrived(seven(rrec.at[k], count_rows), rs_r.at[k])
        total = prec[k, chip, at].astype(F32)
        for e in range(1, 8):
            total = total + rrec[k, chip_at(e), at].astype(F32)
        return total

    def sorted_first(k):
        return (k >= 2) & (k < 8)

    def spread_first(k):
        for e in (1, 3, 2):
            to = rep_at(e)
            send(fr.at[k, rep], fr.at[k, rep], fw_s.at[k], fw_r.at[k], (to, sec, ten))

    def all_first(k):
        arrived(fr.at[k, pl.ds(0, 3)], fw_r.at[k])

    def reduce_first(k):
        total = reduce_rows(k, 16)
        stream = (bnd[pl.ds(0, 16), columns(k)].astype(F32) + total).astype(BF16)
        so[pl.ds(0, 16), columns(k)] = stream
        so[pl.ds(16, 16), columns(k)] = jnp.zeros_like(stream)
        fr[k, rep] = stream

        @pl.when(sorted_first(k))
        def _():
            spread_first(k)

        @pl.when(jnp.logical_not(sorted_first(k)))
        def _():
            send(fr.at[k, rep], fr.at[k, rep], yf_s.at[k], yf_r.at[k], across)

    def reduce_second(k):
        bsum[k] = reduce_rows(k, 32)

    def route_ahead(k):
        @pl.when(jnp.logical_not(sorted_first(k)))
        def _():
            arrived(fr.at[k, rep], yf_r.at[k])
            spread_first(k)

    def sort_first(k):
        @pl.when(sorted_first(k))
        def _():
            all_first(k)
            yb[k] = dot(sel_f[...], fr[k].reshape(64, width)).astype(BF16).reshape(2, 16, width)
            send(yb.at[k], fr.at[k, pl.ds(0, 2)], yf_s.at[k], yf_r.at[k], across)

    def put_second(k, arriving):
        total = arriving + bsum[k]
        so[:, columns(k)] = (total.astype(BF16).astype(F32) * mask[:, 0:1]).astype(BF16)

    def finish_second(k):
        @pl.when(sorted_first(k))
        def _():
            arrived(fr.at[k, pl.ds(0, 2)], yf_r.at[k])
            put_second(k, fr[k, pl.ds(0, 2)].reshape(32, width).astype(F32))

        @pl.when(jnp.logical_not(sorted_first(k)))
        def _():
            all_first(k)
            put_second(k, dot(sel_f[...], fr[k].reshape(64, width)))

    @pl.when(sec == 1)
    def _():
        route_back(0)
        gather_second(0)
        loop(CHUNKS - 1, lambda k: route_back(k + 1))

    cg[...] = jnp.zeros_like(cg)
    ctx_t[...] = ctx[...].reshape(512, 256).T
    sel_f[...] = selector((32, 64), 1, 0)

    @pl.when(sec == 0)
    def _():
        def clear(k):
            loop(8, lambda c: cot.at[k, core, c, pl.ds(16, 16)].__setitem__(..., jnp.zeros((16, width), BF16)))

        loop(CHUNKS, clear)

    def first_sent(k):
        sent(fr.at[k, pl.ds(0, 3)], fw_s.at[k])

    def drain(k):
        def rows_sent(count_rows):
            sent(seven(cot.at[k, core], count_rows), ag_s.at[k])
            sent(seven(prec.at[k], count_rows), rs_s.at[k])

        @pl.when(sec == 0)
        def _():
            rows_sent(16)

            @pl.when(sorted_first(k))
            def _():
                sent(yb.at[k], yf_s.at[k])
                first_sent(k)

            @pl.when(jnp.logical_not(sorted_first(k)))
            def _():
                sent(fr.at[k, rep], yf_s.at[k])

        @pl.when(sec == 1)
        def _():
            rows_sent(32)
            sent(yb.at[k, 0], yb_s.at[k])
            sent(bsend.at[k, pl.ds(0, 3)], bk_s.at[k])

            @pl.when(jnp.logical_not(sorted_first(k)))
            def _():
                first_sent(k)

        sent(cot.at[k, core], cf_s.at[k])
        sent(part.at[k], cp_s.at[k])
        sent(msg.at[k], p1_s.at[k])
        sent(st.at[k], p2_s.at[k])

    late = 1 - sec
    stages = (
        (2, None, lambda k: w_in(k).wait()),
        (2 + late, None, message),
        (4 + late, None, pass_on),
        (1, 0, gather_first),
        (None, 1, cross_back),
        (-1, 1, gather_second),
        (1 + late, None, share),
        (2, None, branch_far),
        (4, None, branch_near),
        (6, 0, reduce_first),
        (6, 1, reduce_second),
        (AHEAD, 1, route_ahead),
        (AHEAD, 0, sort_first),
        (AHEAD + 2, 1, finish_second),
        (2 + late, None, context_part),
        (6 + late, None, update),
        (AHEAD + 2, None, drain),
    )

    def run(live, only, stage, k):
        live = live & (k < CHUNKS)
        if only is not None:
            live = live & (sec == only)
        pl.when(live)(functools.partial(stage, k))

    def step(i):
        for lag, only, stage in stages:
            if lag is None:
                run(i >= 1, only, stage, 2 * i - 1)
                run(i >= 0, only, stage, 2 * i)
            else:
                k = i - lag
                run((k >= 0) & (i >= 0), only, stage, k)

    loop(CHUNKS + AHEAD + 2, step)

    cg_out[...] = cg[...].astype(BF16)


def local(boundary, context, weights, momentum, route, partner):
    beta = BETA_SCALE / math.sqrt(512)
    model = weights.shape[-1]
    width = model // CHUNKS
    bnd = boundary.reshape(8, 4, model).transpose(1, 0, 2).reshape(32, model)
    ctx = context.reshape(8, 2, 8, 4, 256).transpose(1, 0, 3, 2, 4).reshape(2, 256, 256)
    n = CHUNKS
    dma = pltpu.SemaphoreType.DMA
    scratch = [
        pltpu.VMEM((256, 512), BF16),
        pltpu.VMEM((512, 256), F32),
        pltpu.VMEM((n, 2, 8, 32, width), BF16),
        pltpu.VMEM((n, 2, 128, width), BF16),
        pltpu.VMEM((n, 2, 128, width), BF16),
        pltpu.VMEM((n, 2, 128, width), BF16),
        pltpu.VMEM((n, 2, 128, width), BF16),
        pltpu.VMEM((n, 8, 32, width), BF16),
        pltpu.VMEM((n, 8, 32, width), BF16),
        pltpu.VMEM((n, 8, 32, width), BF16),
        pltpu.VMEM((n, 32, width), F32),
        pltpu.VMEM((n, 4, 16, width), BF16),
        pltpu.VMEM((n, 4, 16, width), BF16),
        pltpu.VMEM((n, 4, 16, width), BF16),
        pltpu.VMEM((n, 2, 16, width), BF16),
        pltpu.VMEM((64, 32), BF16),
        pltpu.VMEM((32, 64), BF16),
        pltpu.VMEM((32, 128), F32),
        *[dma((n,))] * 17,
        dma((n, 2)),
        *[dma((n,))] * 4,
    ]
    vmem = pl.BlockSpec(memory_space=pltpu.VMEM)
    smem = pl.BlockSpec(memory_space=pltpu.SMEM)
    anywhere = pl.BlockSpec(memory_space=pl.ANY)
    stream, ctx_grad, new_weights, new_momentum = pl.pallas_call(
        functools.partial(kernel, beta, width),
        out_shape=(
            pltpu.VMEM((32, model), BF16),
            pltpu.VMEM((512, 256), BF16),
            pltpu.VMEM((256, model), BF16),
            pltpu.VMEM((256, model), BF16),
        ),
        in_specs=[smem, smem, vmem, vmem, anywhere, anywhere],
        out_specs=(vmem, vmem, vmem, vmem),
        scratch_shapes=scratch,
        compiler_params=pltpu.CompilerParams(
            collective_id=0, has_side_effects=True, vmem_limit_bytes=48 * 2**20
        ),
        name="noloco_step",
    )(route.T, partner.T, bnd, ctx, weights[0, 0], momentum[0, 0])
    stream = stream.reshape(4, 8, model).transpose(1, 0, 2).reshape(1, 1, 8, 4, model)
    ctx_grad = ctx_grad.reshape(2, 8, 4, 8, 256).transpose(1, 0, 3, 2, 4).reshape(1, 1, 128, 4, 256)
    return stream, ctx_grad, new_weights[None, None], new_momentum[None, None]


def solution(mesh):
    in_specs = (
        P("replica", "section", "tensor", None, None),
        P("replica", "section", None, None, "tensor"),
        P("replica", "section", "tensor", None),
        P("replica", "section", "tensor", None),
        P(),
        P(),
    )
    out_specs = (
        P("replica", "section", "tensor", None, None),
        P("replica", "section", None, None, "tensor"),
        P("replica", "section", "tensor", None),
        P("replica", "section", "tensor", None),
    )
    return jax.shard_map(local, mesh=mesh, in_specs=in_specs, out_specs=out_specs, check_vma=False)
```

```python
import functools
import math

import jax
import jax.numpy as jnp
from jax import lax
from jax.experimental import pallas as pl
from jax.experimental.pallas import tpu as pltpu
from jax.sharding import PartitionSpec as P

ALPHA = 0.9
GAMMA = 0.5
BETA_SCALE = 0.4
CHUNKS = 16
AHEAD = 8
TILE = 512
MESH = pl.DeviceIdType.MESH
BF16 = jnp.bfloat16
F32 = jnp.float32


def loop(n, body):
    def step(i, carry):
        body(i)
        return carry

    lax.fori_loop(0, n, step, 0)


def by_slot(block):
    return jnp.swapaxes(block.astype(F32), 0, 1).reshape(-1, block.shape[-1])


def by_token(rows):
    return jnp.swapaxes(rows.reshape(4, 8, rows.shape[-1]), 0, 1).astype(BF16)


def dot(a, b):
    return jnp.dot(a, b, preferred_element_type=F32)


def kernel(
    beta, width, route, partner, own, ctx_hbm, w_hbm, m_hbm, so, cg_out, w, mom,
    bnd, ctx_in_order, ctx, ctx_t, cg, cot, msg, g1, st, g2, part, prec, rrec, bsum, bsend, brecv, fr, yb, sel_b, sel_f, mask,
    ag_s, ag_r, rs_s, rs_r, bk_s, bk_r, fw_s, fw_r, yb_s, yb_r, yf_s, yf_r, cf_s, cf_r, cp_s, cp_r,
    p1_s, p1_r, p2_s, p2_r, w_i, m_i, c_i,
):
    rep = lax.axis_index("replica")
    sec = lax.axis_index("section")
    ten = lax.axis_index("tensor")
    chip = lax.div(ten, 2)
    core = lax.rem(ten, 2)
    z = lax.div(chip, 2)
    high = lax.rem(chip, 2)
    other = 1 - core
    sibling = (rep, sec, 2 * chip + other)
    right = (lax.rem(rep + 1, 4), sec, ten)
    left = (lax.rem(rep + 3, 4), sec, ten)
    across = (rep, 1 - sec, ten)

    def chip_at(e):
        return lax.rem(z + lax.div(e, 2), 4) * 2 + lax.rem(high + lax.rem(e, 2), 2)

    def rep_at(e):
        return lax.rem(rep + e, 4)

    def peer(e):
        return (rep, sec, 2 * chip_at(e) + core)

    def send(src, dst, ss, rs, to):
        pltpu.make_async_remote_copy(
            src_ref=src, dst_ref=dst, send_sem=ss, recv_sem=rs, device_id=to, device_id_type=MESH
        ).start()

    def sent(ref, sem):
        pltpu.make_async_remote_copy(
            src_ref=ref, dst_ref=ref, send_sem=sem, recv_sem=sem, device_id=sibling, device_id_type=MESH
        ).wait_send()

    def arrived(ref, sem):
        pltpu.make_async_remote_copy(
            src_ref=ref, dst_ref=ref, send_sem=sem, recv_sem=sem, device_id=sibling, device_id_type=MESH
        ).wait_recv()

    def seven(ref, count_rows):
        return ref.at[pl.ds(0, 7), pl.ds(0, count_rows)]

    def columns(k):
        return pl.ds(pl.multiple_of(k * width, width), width)

    def tiles(body):
        loop(width // TILE, lambda j: body(pl.ds(pl.multiple_of(j * TILE, TILE), TILE)))

    def model(k, body):
        def one(j):
            whole = pl.multiple_of(k * width + j * TILE, TILE)
            body(pl.ds(pl.multiple_of(j * TILE, TILE), TILE), pl.ds(whole, TILE))

        loop(width // TILE, one)

    w_in = pltpu.make_async_copy(w_hbm, w, w_i)
    m_in = pltpu.make_async_copy(m_hbm, mom, m_i)
    ctx_in = pltpu.make_async_copy(ctx_hbm, ctx_in_order, c_i)

    barrier = pltpu.get_barrier_semaphore()

    def greet(to):
        pl.semaphore_signal(barrier, inc=1, device_id=to, device_id_type=MESH)

    greet(sibling)
    greet(across)
    for e in range(1, 4):
        greet((rep_at(e), sec, ten))
    loop(7, lambda e: greet(peer(e + 1)))
    ctx_in.start()
    w_in.start()

    routes = [route[j % 2, j // 2] for j in range(8)]
    slots = []
    for j in range(8):
        before = jnp.int32(0)
        for i in range(j):
            before = before + jnp.where(routes[i] == routes[j], 1, 0)
        slots.append(before)
    count = jnp.int32(0)
    for j in range(8):
        count = count + jnp.where(routes[j] == rep, 1, 0)

    def selector(shape, wide, narrow):
        a = lax.broadcasted_iota(jnp.int32, shape, wide)
        b = lax.broadcasted_iota(jnp.int32, shape, narrow)
        same = jnp.where(a % 8 == b % 8, 1.0, 0.0)
        pair, slot = a // 8, b // 8
        total = jnp.zeros(shape, F32)
        for j in range(8):
            mine = jnp.where(routes[j] == rep, 1.0, 0.0).astype(F32)
            total = total + mine * jnp.where((pair == j) & (slot == slots[j]), same, 0.0)
        return total.astype(BF16)

    sel_b[...] = selector((64, 32), 0, 1)
    rows = lax.broadcasted_iota(jnp.int32, (32, 128), 0)
    mask[...] = jnp.where(rows // 8 < count, 1.0, 0.0)

    as_one = lambda flag: jnp.where(flag, 1.0, 0.0).astype(F32)
    own_right = as_one(partner[sec, rep_at(1)] == rep)
    own_left = as_one(partner[sec, rep_at(3)] == rep)
    mine = partner[sec, rep]
    from_left = as_one(mine == rep_at(3))
    from_right = as_one(mine == rep_at(1))
    from_far = as_one(mine == rep_at(2))

    pl.semaphore_wait(barrier, 12)

    def gather(k, count_rows):
        block = cot.at[k, core, chip, pl.ds(0, count_rows)]
        loop(7, lambda e: send(block, block, ag_s.at[k], ag_r.at[k], peer(e + 1)))

    def route_back(k):
        bnd[:, columns(k)] = by_slot(own[:, :, columns(k)]).astype(BF16)
        bsend[k] = dot(sel_b[...], bnd[:, columns(k)]).astype(BF16).reshape(4, 16, width)
        for e in (1, 3, 2):
            to = rep_at(e)
            send(bsend.at[k, to], brecv.at[k, rep], bk_s.at[k], bk_r.at[k], (to, sec, ten))

    def cross_back(k):
        total = bsend[k, rep].astype(F32)
        arrived(brecv.at[k, pl.ds(0, 3)], bk_r.at[k])
        for e in (1, 3, 2):
            total = total + brecv[k, rep_at(e)].astype(F32)
        yb[k, 0] = total.astype(BF16)
        send(yb.at[k, 0], cot.at[k, core, chip, pl.ds(0, 16)], yb_s.at[k], yb_r.at[k], across)

    def gather_first(k):
        arrived(cot.at[k, core, chip, pl.ds(0, 16)], yb_r.at[k])
        gather(k, 16)

    def gather_second(k):
        cot[k, core, chip] = (bnd[:, columns(k)].astype(F32) * mask[:, 0:1]).astype(BF16)
        gather(k, 32)

    def share(k):
        pl.when(sec == 0)(lambda: arrived(seven(cot.at[k, core], 16), ag_r.at[k]))
        pl.when(sec == 1)(lambda: arrived(seven(cot.at[k, core], 32), ag_r.at[k]))
        send(cot.at[k, core], cot.at[k, core], cf_s.at[k], cf_r.at[k], sibling)

    def cot_tile(k, cols):
        return cot[k, :, :, :, cols].reshape(512, TILE)

    def message(k):
        arrived(cot.at[k, other], cf_r.at[k])

        def one(cols, whole):
            grad = dot(ctx_t[...], cot_tile(k, cols))
            out = beta * grad - GAMMA * w[:, whole].astype(F32)
            msg[k, :, :, cols] = out.astype(BF16).reshape(2, 128, TILE)

        model(k, one)
        send(msg.at[k, 0], g1.at[k, 0], p1_s.at[k], p1_r.at[k, 0], right)
        send(msg.at[k, 1], g1.at[k, 1], p1_s.at[k], p1_r.at[k, 1], left)

    def context_part(k):
        def one(cols, whole):
            cg[...] += lax.dot_general(
                cot_tile(k, cols), w[:, whole], (((1,), (1,)), ((), ())), preferred_element_type=F32
            )

        model(k, one)

    def pass_on(k):
        arrived(g1.at[k, 0], p1_r.at[k, 0])

        def one(cols):
            mixed = own_right * msg[k, 1, :, cols].astype(F32) + (1.0 - own_right) * g1[k, 0, :, cols].astype(F32)
            st[k, 0, :, cols] = mixed.astype(BF16)

        tiles(one)
        send(st.at[k, 0], g2.at[k, 0], p2_s.at[k], p2_r.at[k], right)
        arrived(g1.at[k, 1], p1_r.at[k, 1])

        def two(cols):
            mixed = own_left * msg[k, 0, :, cols].astype(F32) + (1.0 - own_left) * g1[k, 1, :, cols].astype(F32)
            st[k, 1, :, cols] = mixed.astype(BF16)

        tiles(two)
        send(st.at[k, 1], g2.at[k, 1], p2_s.at[k], p2_r.at[k], left)

    def update(k):
        arrived(g2.at[k], p2_r.at[k])

        def one(cols, whole):
            grad = dot(ctx_t[...], cot_tile(k, cols))
            a1, b1 = g1[k, 0, :, cols].astype(F32), g1[k, 1, :, cols].astype(F32)
            a2, b2 = g2[k, 0, :, cols].astype(F32), g2[k, 1, :, cols].astype(F32)
            top = from_left * a1 + from_right * b2 + from_far * a2
            low = from_left * a2 + from_right * b1 + from_far * b2
            for half, theirs in ((0, top), (128, low)):
                at = pl.ds(half, 128)
                current = w[at, whole].astype(F32)
                delta = (
                    ALPHA * mom[at, whole].astype(F32)
                    - 0.5 * (beta * grad[half : half + 128] + GAMMA * current)
                    - 0.5 * theirs
                )
                mom[at, whole] = delta.astype(BF16)
                w[at, whole] = (current + delta).astype(BF16)

        model(k, one)

    def first_update(k):
        pl.when(k == 0)(lambda: m_in.wait())
        update(k)

    def branch_far(k):
        def one(cols, whole):
            part[k, :, :, cols] = dot(ctx[other], w[:, whole]).astype(BF16).reshape(8, 32, TILE)

        model(k, one)
        send(part.at[k], prec.at[k], cp_s.at[k], cp_r.at[k], sibling)

    def branch_near(k):
        arrived(prec.at[k], cp_r.at[k])

        def one(cols, whole):
            own = dot(ctx[core], w[:, whole]).reshape(8, 32, TILE)
            prec[k, :, :, cols] = (own + prec[k, :, :, cols].astype(F32)).astype(BF16)

        model(k, one)

        def spread(count_rows):
            def one_peer(e):
                block = prec.at[k, chip_at(e + 1), pl.ds(0, count_rows)]
                to = rrec.at[k, chip, pl.ds(0, count_rows)]
                send(block, to, rs_s.at[k], rs_r.at[k], peer(e + 1))

            loop(7, one_peer)

        pl.when(sec == 0)(lambda: spread(16))
        pl.when(sec == 1)(lambda: spread(32))

    def reduce_rows(k, count_rows):
        at = pl.ds(0, count_rows)

        arrived(seven(rrec.at[k], count_rows), rs_r.at[k])
        total = prec[k, chip, at].astype(F32)
        for e in range(1, 8):
            total = total + rrec[k, chip_at(e), at].astype(F32)
        return total

    def sorted_first(k):
        return (k >= 2) & (k < 8)

    def spread_first(k):
        for e in (1, 3, 2):
            to = rep_at(e)
            send(fr.at[k, rep], fr.at[k, rep], fw_s.at[k], fw_r.at[k], (to, sec, ten))

    def all_first(k):
        arrived(fr.at[k, pl.ds(0, 3)], fw_r.at[k])

    def reduce_first(k):
        total = reduce_rows(k, 16)
        stream = (by_slot(own[:, :, columns(k)])[0:16] + total).astype(BF16)
        wide = stream.astype(F32)
        so[:, :, columns(k)] = by_token(jnp.concatenate([wide, jnp.zeros_like(wide)], axis=0))
        fr[k, rep] = stream

        @pl.when(sorted_first(k))
        def _():
            spread_first(k)

        @pl.when(jnp.logical_not(sorted_first(k)))
        def _():
            send(fr.at[k, rep], fr.at[k, rep], yf_s.at[k], yf_r.at[k], across)

    def reduce_second(k):
        bsum[k] = reduce_rows(k, 32)

    def route_ahead(k):
        @pl.when(jnp.logical_not(sorted_first(k)))
        def _():
            arrived(fr.at[k, rep], yf_r.at[k])
            spread_first(k)

    def sort_first(k):
        @pl.when(sorted_first(k))
        def _():
            all_first(k)
            yb[k] = dot(sel_f[...], fr[k].reshape(64, width)).astype(BF16).reshape(2, 16, width)
            send(yb.at[k], fr.at[k, pl.ds(0, 2)], yf_s.at[k], yf_r.at[k], across)

    def put_second(k, arriving):
        total = arriving + bsum[k]
        so[:, :, columns(k)] = by_token(total.astype(BF16).astype(F32) * mask[:, 0:1])

    def finish_second(k):
        @pl.when(sorted_first(k))
        def _():
            arrived(fr.at[k, pl.ds(0, 2)], yf_r.at[k])
            put_second(k, fr[k, pl.ds(0, 2)].reshape(32, width).astype(F32))

        @pl.when(jnp.logical_not(sorted_first(k)))
        def _():
            all_first(k)
            put_second(k, dot(sel_f[...], fr[k].reshape(64, width)))

    @pl.when(sec == 1)
    def _():
        route_back(0)
        gather_second(0)
        loop(CHUNKS - 1, lambda k: route_back(k + 1))

    m_in.start()
    cg[...] = jnp.zeros_like(cg)
    ctx_in.wait()

    def order_rows(t):
        block = by_slot(ctx_in_order[pl.ds(t * 8, 8)]).astype(BF16)
        ctx[lax.rem(t, 2), pl.ds(pl.multiple_of(lax.div(t, 2) * 32, 32), 32)] = block

    loop(16, order_rows)
    ctx_t[...] = ctx[...].reshape(512, 256).T
    sel_f[...] = selector((32, 64), 1, 0)

    @pl.when(sec == 0)
    def _():
        def clear(k):
            loop(8, lambda c: cot.at[k, core, c, pl.ds(16, 16)].__setitem__(..., jnp.zeros((16, width), BF16)))

        loop(CHUNKS, clear)

    def first_sent(k):
        sent(fr.at[k, pl.ds(0, 3)], fw_s.at[k])

    def drain(k):
        def rows_sent(count_rows):
            sent(seven(cot.at[k, core], count_rows), ag_s.at[k])
            sent(seven(prec.at[k], count_rows), rs_s.at[k])

        @pl.when(sec == 0)
        def _():
            rows_sent(16)

            @pl.when(sorted_first(k))
            def _():
                sent(yb.at[k], yf_s.at[k])
                first_sent(k)

            @pl.when(jnp.logical_not(sorted_first(k)))
            def _():
                sent(fr.at[k, rep], yf_s.at[k])

        @pl.when(sec == 1)
        def _():
            rows_sent(32)
            sent(yb.at[k, 0], yb_s.at[k])
            sent(bsend.at[k, pl.ds(0, 3)], bk_s.at[k])

            @pl.when(jnp.logical_not(sorted_first(k)))
            def _():
                first_sent(k)

        sent(cot.at[k, core], cf_s.at[k])
        sent(part.at[k], cp_s.at[k])
        sent(msg.at[k], p1_s.at[k])
        sent(st.at[k], p2_s.at[k])

    w_in.wait()
    late = 1 - sec
    stages = (
        (2 + late, None, message),
        (4 + late, None, pass_on),
        (1, 0, gather_first),
        (None, 1, cross_back),
        (-1, 1, gather_second),
        (1 + late, None, share),
        (2, None, branch_far),
        (4, None, branch_near),
        (6, 0, reduce_first),
        (6, 1, reduce_second),
        (AHEAD, 1, route_ahead),
        (AHEAD, 0, sort_first),
        (AHEAD + 2, 1, finish_second),
        (2 + late, None, context_part),
        (6 + late, None, first_update),
        (AHEAD + 2, None, drain),
    )

    def put_context(t):
        row = (lax.rem(t, 2) * 8 + lax.div(t, 2)) * 32
        cg_out[pl.ds(t * 8, 8)] = by_token(cg[pl.ds(pl.multiple_of(row, 32), 32)])

    def run(live, only, stage, k):
        live = live & (k < CHUNKS)
        if only is not None:
            live = live & (sec == only)
        pl.when(live)(functools.partial(stage, k))

    def step(i):
        pl.when(i == CHUNKS + 4)(lambda: loop(16, put_context))

        for lag, only, stage in stages:
            if lag is None:
                run(i >= 1, only, stage, 2 * i - 1)
                run(i >= 0, only, stage, 2 * i)
            else:
                k = i - lag
                run((k >= 0) & (i >= 0), only, stage, k)

    loop(CHUNKS + AHEAD + 2, step)


def local(boundary, context, weights, momentum, route, partner):
    beta = BETA_SCALE / math.sqrt(512)
    model = weights.shape[-1]
    width = model // CHUNKS
    n = CHUNKS
    dma = pltpu.SemaphoreType.DMA
    scratch = [
        pltpu.VMEM((32, model), BF16),
        pltpu.VMEM((128, 4, 256), BF16),
        pltpu.VMEM((2, 256, 256), BF16),
        pltpu.VMEM((256, 512), BF16),
        pltpu.VMEM((512, 256), F32),
        pltpu.VMEM((n, 2, 8, 32, width), BF16),
        pltpu.VMEM((n, 2, 128, width), BF16),
        pltpu.VMEM((n, 2, 128, width), BF16),
        pltpu.VMEM((n, 2, 128, width), BF16),
        pltpu.VMEM((n, 2, 128, width), BF16),
        pltpu.VMEM((n, 8, 32, width), BF16),
        pltpu.VMEM((n, 8, 32, width), BF16),
        pltpu.VMEM((n, 8, 32, width), BF16),
        pltpu.VMEM((n, 32, width), F32),
        pltpu.VMEM((n, 4, 16, width), BF16),
        pltpu.VMEM((n, 4, 16, width), BF16),
        pltpu.VMEM((n, 4, 16, width), BF16),
        pltpu.VMEM((n, 2, 16, width), BF16),
        pltpu.VMEM((64, 32), BF16),
        pltpu.VMEM((32, 64), BF16),
        pltpu.VMEM((32, 128), F32),
        *[dma((n,))] * 17,
        dma((n, 2)),
        *[dma((n,))] * 2,
        *[dma] * 3,
    ]
    vmem = pl.BlockSpec(memory_space=pltpu.VMEM)
    smem = pl.BlockSpec(memory_space=pltpu.SMEM)
    anywhere = pl.BlockSpec(memory_space=pl.ANY)
    stream, ctx_grad, new_weights, new_momentum = pl.pallas_call(
        functools.partial(kernel, beta, width),
        out_shape=(
            pltpu.VMEM((8, 4, model), BF16),
            pltpu.VMEM((128, 4, 256), BF16),
            pltpu.VMEM((256, model), BF16),
            pltpu.VMEM((256, model), BF16),
        ),
        in_specs=[smem, smem, vmem, anywhere, anywhere, anywhere],
        out_specs=(vmem, vmem, vmem, vmem),
        scratch_shapes=scratch,
        compiler_params=pltpu.CompilerParams(
            collective_id=0, has_side_effects=True, vmem_limit_bytes=50 * 2**20
        ),
        name="noloco_step",
    )(route.T, partner.T, boundary[0, 0], context[0, 0], weights[0, 0], momentum[0, 0])
    return stream[None, None], ctx_grad[None, None], new_weights[None, None], new_momentum[None, None]


def solution(mesh):
    in_specs = (
        P("replica", "section", "tensor", None, None),
        P("replica", "section", None, None, "tensor"),
        P("replica", "section", "tensor", None),
        P("replica", "section", "tensor", None),
        P(),
        P(),
    )
    out_specs = (
        P("replica", "section", "tensor", None, None),
        P("replica", "section", None, None, "tensor"),
        P("replica", "section", "tensor", None),
        P("replica", "section", "tensor", None),
    )
    return jax.shard_map(local, mesh=mesh, in_specs=in_specs, out_specs=out_specs, check_vma=False)
```

```python
import functools
import math

import jax
import jax.numpy as jnp
from jax import lax
from jax.experimental import pallas as pl
from jax.experimental.pallas import tpu as pltpu
from jax.sharding import PartitionSpec as P

ALPHA = 0.9
GAMMA = 0.5
BETA_SCALE = 0.4
CHUNKS = 16
AHEAD = 8
TILE = 512
MESH = pl.DeviceIdType.MESH
BF16 = jnp.bfloat16
F32 = jnp.float32


def loop(n, body):
    def step(i, carry):
        body(i)
        return carry

    lax.fori_loop(0, n, step, 0)


def by_slot(block):
    return jnp.swapaxes(block.astype(F32), 0, 1).reshape(-1, block.shape[-1])


def by_token(rows):
    return jnp.swapaxes(rows.reshape(4, 8, rows.shape[-1]), 0, 1).astype(BF16)


def dot(a, b):
    return jnp.dot(a, b, preferred_element_type=F32)


def kernel(
    beta, width, route, partner, own_hbm, ctx_hbm, w_hbm, m_hbm, so, cg_out, w, mom,
    own, bnd, ctx_in_order, ctx, ctx_t, cg, cot, msg, g1, st, g2, part, prec, rrec, bsum, bsend, brecv, fr, yb, sel_b, sel_f, mask,
    ag_s, ag_r, rs_s, rs_r, bk_s, bk_r, fw_s, fw_r, yb_s, yb_r, yf_s, yf_r, cf_s, cf_r, cp_s, cp_r,
    p1_s, p1_r, p2_s, p2_r, w_i, m_i, c_i, b_i,
):
    rep = lax.axis_index("replica")
    sec = lax.axis_index("section")
    ten = lax.axis_index("tensor")
    chip = lax.div(ten, 2)
    core = lax.rem(ten, 2)
    z = lax.div(chip, 2)
    high = lax.rem(chip, 2)
    other = 1 - core
    sibling = (rep, sec, 2 * chip + other)
    right = (lax.rem(rep + 1, 4), sec, ten)
    left = (lax.rem(rep + 3, 4), sec, ten)
    across = (rep, 1 - sec, ten)

    def chip_at(e):
        return lax.rem(z + lax.div(e, 2), 4) * 2 + lax.rem(high + lax.rem(e, 2), 2)

    def rep_at(e):
        return lax.rem(rep + e, 4)

    def peer(e):
        return (rep, sec, 2 * chip_at(e) + core)

    def send(src, dst, ss, rs, to):
        pltpu.make_async_remote_copy(
            src_ref=src, dst_ref=dst, send_sem=ss, recv_sem=rs, device_id=to, device_id_type=MESH
        ).start()

    def sent(ref, sem):
        pltpu.make_async_remote_copy(
            src_ref=ref, dst_ref=ref, send_sem=sem, recv_sem=sem, device_id=sibling, device_id_type=MESH
        ).wait_send()

    def arrived(ref, sem):
        pltpu.make_async_remote_copy(
            src_ref=ref, dst_ref=ref, send_sem=sem, recv_sem=sem, device_id=sibling, device_id_type=MESH
        ).wait_recv()

    def seven(ref, count_rows):
        return ref.at[pl.ds(0, 7), pl.ds(0, count_rows)]

    def columns(k):
        return pl.ds(pl.multiple_of(k * width, width), width)

    def tiles(body):
        loop(width // TILE, lambda j: body(pl.ds(pl.multiple_of(j * TILE, TILE), TILE)))

    def model(k, body):
        def one(j):
            whole = pl.multiple_of(k * width + j * TILE, TILE)
            body(pl.ds(pl.multiple_of(j * TILE, TILE), TILE), pl.ds(whole, TILE))

        loop(width // TILE, one)

    w_in = pltpu.make_async_copy(w_hbm, w, w_i)
    m_in = pltpu.make_async_copy(m_hbm, mom, m_i)
    ctx_in = pltpu.make_async_copy(ctx_hbm, ctx_in_order, c_i)

    own_in = pltpu.make_async_copy(own_hbm, own, b_i)
    own_in.start()
    barrier = pltpu.get_barrier_semaphore()

    def greet(to):
        pl.semaphore_signal(barrier, inc=1, device_id=to, device_id_type=MESH)

    greet(sibling)
    greet(across)
    for e in range(1, 4):
        greet((rep_at(e), sec, ten))
    loop(7, lambda e: greet(peer(e + 1)))
    ctx_in.start()
    w_in.start()

    routes = [route[j % 2, j // 2] for j in range(8)]
    slots = []
    for j in range(8):
        before = jnp.int32(0)
        for i in range(j):
            before = before + jnp.where(routes[i] == routes[j], 1, 0)
        slots.append(before)
    count = jnp.int32(0)
    for j in range(8):
        count = count + jnp.where(routes[j] == rep, 1, 0)

    def selector(shape, wide, narrow):
        a = lax.broadcasted_iota(jnp.int32, shape, wide)
        b = lax.broadcasted_iota(jnp.int32, shape, narrow)
        same = jnp.where(a % 8 == b % 8, 1.0, 0.0)
        pair, slot = a // 8, b // 8
        total = jnp.zeros(shape, F32)
        for j in range(8):
            mine = jnp.where(routes[j] == rep, 1.0, 0.0).astype(F32)
            total = total + mine * jnp.where((pair == j) & (slot == slots[j]), same, 0.0)
        return total.astype(BF16)

    sel_b[...] = selector((64, 32), 0, 1)
    rows = lax.broadcasted_iota(jnp.int32, (32, 128), 0)
    mask[...] = jnp.where(rows // 8 < count, 1.0, 0.0)

    as_one = lambda flag: jnp.where(flag, 1.0, 0.0).astype(F32)
    own_right = as_one(partner[sec, rep_at(1)] == rep)
    own_left = as_one(partner[sec, rep_at(3)] == rep)
    mine = partner[sec, rep]
    from_left = as_one(mine == rep_at(3))
    from_right = as_one(mine == rep_at(1))
    from_far = as_one(mine == rep_at(2))

    own_in.wait()
    pl.semaphore_wait(barrier, 12)

    def gather(k, count_rows):
        block = cot.at[k, core, chip, pl.ds(0, count_rows)]
        loop(7, lambda e: send(block, block, ag_s.at[k], ag_r.at[k], peer(7 - e)))

    def route_back(k):
        bnd[:, columns(k)] = by_slot(own[:, :, columns(k)]).astype(BF16)
        bsend[k] = dot(sel_b[...], bnd[:, columns(k)]).astype(BF16).reshape(4, 16, width)
        for e in (1, 3, 2):
            to = rep_at(e)
            send(bsend.at[k, to], brecv.at[k, rep], bk_s.at[k], bk_r.at[k], (to, sec, ten))

    def cross_back(k):
        total = bsend[k, rep].astype(F32)
        arrived(brecv.at[k, pl.ds(0, 3)], bk_r.at[k])
        for e in (1, 3, 2):
            total = total + brecv[k, rep_at(e)].astype(F32)
        yb[k, 0] = total.astype(BF16)
        send(yb.at[k, 0], cot.at[k, core, chip, pl.ds(0, 16)], yb_s.at[k], yb_r.at[k], across)

    def gather_first(k):
        arrived(cot.at[k, core, chip, pl.ds(0, 16)], yb_r.at[k])
        gather(k, 16)

    def gather_second(k):
        cot[k, core, chip] = (bnd[:, columns(k)].astype(F32) * mask[:, 0:1]).astype(BF16)
        gather(k, 32)

    def share(k):
        pl.when(sec == 0)(lambda: arrived(seven(cot.at[k, core], 16), ag_r.at[k]))
        pl.when(sec == 1)(lambda: arrived(seven(cot.at[k, core], 32), ag_r.at[k]))
        send(cot.at[k, core], cot.at[k, core], cf_s.at[k], cf_r.at[k], sibling)

    def cot_tile(k, cols):
        return cot[k, :, :, :, cols].reshape(512, TILE)

    def message(k):
        arrived(cot.at[k, other], cf_r.at[k])

        def one(half, cols, whole):
            at = pl.ds(half * 128, 128)
            grad = dot(ctx_t[at, :], cot_tile(k, cols))
            out = beta * grad - GAMMA * w[at, whole].astype(F32)
            msg[k, half, :, cols] = out.astype(BF16)

        for half, to in ((0, right), (1, left)):
            model(k, functools.partial(one, half))
            send(msg.at[k, half], g1.at[k, half], p1_s.at[k], p1_r.at[k, half], to)

    def context_part(k):
        def one(cols, whole):
            cg[...] += lax.dot_general(
                cot_tile(k, cols), w[:, whole], (((1,), (1,)), ((), ())), preferred_element_type=F32
            )

        model(k, one)

    def pass_on(k):
        arrived(g1.at[k, 0], p1_r.at[k, 0])

        def one(cols):
            mixed = own_right * msg[k, 1, :, cols].astype(F32) + (1.0 - own_right) * g1[k, 0, :, cols].astype(F32)
            st[k, 0, :, cols] = mixed.astype(BF16)

        tiles(one)
        send(st.at[k, 0], g2.at[k, 0], p2_s.at[k], p2_r.at[k], right)
        arrived(g1.at[k, 1], p1_r.at[k, 1])

        def two(cols):
            mixed = own_left * msg[k, 0, :, cols].astype(F32) + (1.0 - own_left) * g1[k, 1, :, cols].astype(F32)
            st[k, 1, :, cols] = mixed.astype(BF16)

        tiles(two)
        send(st.at[k, 1], g2.at[k, 1], p2_s.at[k], p2_r.at[k], left)

    def update(k):
        arrived(g2.at[k], p2_r.at[k])

        def one(cols, whole):
            grad = dot(ctx_t[...], cot_tile(k, cols))
            a1, b1 = g1[k, 0, :, cols].astype(F32), g1[k, 1, :, cols].astype(F32)
            a2, b2 = g2[k, 0, :, cols].astype(F32), g2[k, 1, :, cols].astype(F32)
            top = from_left * a1 + from_right * b2 + from_far * a2
            low = from_left * a2 + from_right * b1 + from_far * b2
            for half, theirs in ((0, top), (128, low)):
                at = pl.ds(half, 128)
                current = w[at, whole].astype(F32)
                delta = (
                    ALPHA * mom[at, whole].astype(F32)
                    - 0.5 * (beta * grad[half : half + 128] + GAMMA * current)
                    - 0.5 * theirs
                )
                mom[at, whole] = delta.astype(BF16)
                w[at, whole] = (current + delta).astype(BF16)

        model(k, one)

    def first_update(k):
        pl.when(k == 0)(lambda: m_in.wait())
        update(k)

    def branch_far(k):
        def one(cols, whole):
            part[k, :, :, cols] = dot(ctx[other], w[:, whole]).astype(BF16).reshape(8, 32, TILE)

        model(k, one)
        send(part.at[k], prec.at[k], cp_s.at[k], cp_r.at[k], sibling)

    def branch_near(k):
        arrived(prec.at[k], cp_r.at[k])

        def one(cols, whole):
            own = dot(ctx[core], w[:, whole]).reshape(8, 32, TILE)
            prec[k, :, :, cols] = (own + prec[k, :, :, cols].astype(F32)).astype(BF16)

        model(k, one)

        def spread(count_rows):
            def one_peer(e):
                block = prec.at[k, chip_at(e + 1), pl.ds(0, count_rows)]
                to = rrec.at[k, chip, pl.ds(0, count_rows)]
                send(block, to, rs_s.at[k], rs_r.at[k], peer(e + 1))

            loop(7, one_peer)

        pl.when(sec == 0)(lambda: spread(16))
        pl.when(sec == 1)(lambda: spread(32))

    def reduce_rows(k, count_rows):
        at = pl.ds(0, count_rows)

        arrived(seven(rrec.at[k], count_rows), rs_r.at[k])
        total = prec[k, chip, at].astype(F32)
        for e in range(1, 8):
            total = total + rrec[k, chip_at(e), at].astype(F32)
        return total

    def sorted_first(k):
        return (k >= 2) & (k < 8)

    def spread_first(k):
        for e in (1, 3, 2):
            to = rep_at(e)
            send(fr.at[k, rep], fr.at[k, rep], fw_s.at[k], fw_r.at[k], (to, sec, ten))

    def all_first(k):
        arrived(fr.at[k, pl.ds(0, 3)], fw_r.at[k])

    def reduce_first(k):
        total = reduce_rows(k, 16)
        stream = (by_slot(own[:, :, columns(k)])[0:16] + total).astype(BF16)
        wide = stream.astype(F32)
        so[:, :, columns(k)] = by_token(jnp.concatenate([wide, jnp.zeros_like(wide)], axis=0))
        fr[k, rep] = stream

        @pl.when(sorted_first(k))
        def _():
            spread_first(k)

        @pl.when(jnp.logical_not(sorted_first(k)))
        def _():
            send(fr.at[k, rep], fr.at[k, rep], yf_s.at[k], yf_r.at[k], across)

    def reduce_second(k):
        bsum[k] = reduce_rows(k, 32)

    def route_ahead(k):
        @pl.when(jnp.logical_not(sorted_first(k)))
        def _():
            arrived(fr.at[k, rep], yf_r.at[k])
            spread_first(k)

    def sort_first(k):
        @pl.when(sorted_first(k))
        def _():
            all_first(k)
            yb[k] = dot(sel_f[...], fr[k].reshape(64, width)).astype(BF16).reshape(2, 16, width)
            send(yb.at[k], fr.at[k, pl.ds(0, 2)], yf_s.at[k], yf_r.at[k], across)

    def put_second(k, arriving):
        total = arriving + bsum[k]
        so[:, :, columns(k)] = by_token(total.astype(BF16).astype(F32) * mask[:, 0:1])

    def finish_second(k):
        @pl.when(sorted_first(k))
        def _():
            arrived(fr.at[k, pl.ds(0, 2)], yf_r.at[k])
            put_second(k, fr[k, pl.ds(0, 2)].reshape(32, width).astype(F32))

        @pl.when(jnp.logical_not(sorted_first(k)))
        def _():
            all_first(k)
            put_second(k, dot(sel_f[...], fr[k].reshape(64, width)))

    @pl.when(sec == 1)
    def _():
        route_back(0)
        gather_second(0)
        loop(CHUNKS - 1, lambda k: route_back(k + 1))

    m_in.start()
    cg[...] = jnp.zeros_like(cg)
    ctx_in.wait()

    def order_rows(t):
        block = by_slot(ctx_in_order[pl.ds(t * 8, 8)]).astype(BF16)
        ctx[lax.rem(t, 2), pl.ds(pl.multiple_of(lax.div(t, 2) * 32, 32), 32)] = block

    loop(16, order_rows)
    ctx_t[...] = ctx[...].reshape(512, 256).T
    sel_f[...] = selector((32, 64), 1, 0)

    @pl.when(sec == 0)
    def _():
        def clear(k):
            loop(8, lambda c: cot.at[k, core, c, pl.ds(16, 16)].__setitem__(..., jnp.zeros((16, width), BF16)))

        loop(CHUNKS, clear)

    def first_sent(k):
        sent(fr.at[k, pl.ds(0, 3)], fw_s.at[k])

    def drain(k):
        def rows_sent(count_rows):
            sent(seven(cot.at[k, core], count_rows), ag_s.at[k])
            sent(seven(prec.at[k], count_rows), rs_s.at[k])

        @pl.when(sec == 0)
        def _():
            rows_sent(16)

            @pl.when(sorted_first(k))
            def _():
                sent(yb.at[k], yf_s.at[k])
                first_sent(k)

            @pl.when(jnp.logical_not(sorted_first(k)))
            def _():
                sent(fr.at[k, rep], yf_s.at[k])

        @pl.when(sec == 1)
        def _():
            rows_sent(32)
            sent(yb.at[k, 0], yb_s.at[k])
            sent(bsend.at[k, pl.ds(0, 3)], bk_s.at[k])

            @pl.when(jnp.logical_not(sorted_first(k)))
            def _():
                first_sent(k)

        sent(cot.at[k, core], cf_s.at[k])
        sent(part.at[k], cp_s.at[k])
        sent(msg.at[k], p1_s.at[k])
        sent(st.at[k], p2_s.at[k])

    w_in.wait()
    late = 1 - sec
    stages = (
        (2 + late, None, message),
        (4 + late, None, pass_on),
        (1, 0, gather_first),
        (None, 1, cross_back),
        (-1, 1, gather_second),
        (1 + late, None, share),
        (2, None, branch_far),
        (4, None, branch_near),
        (6, 0, reduce_first),
        (6, 1, reduce_second),
        (AHEAD, 1, route_ahead),
        (AHEAD, 0, sort_first),
        (AHEAD + 2, 1, finish_second),
        (2 + late, None, context_part),
        (6 + late, None, first_update),
        (AHEAD + 2, None, drain),
    )

    def put_context(t):
        row = (lax.rem(t, 2) * 8 + lax.div(t, 2)) * 32
        cg_out[pl.ds(t * 8, 8)] = by_token(cg[pl.ds(pl.multiple_of(row, 32), 32)])

    def run(live, only, stage, k):
        live = live & (k < CHUNKS)
        if only is not None:
            live = live & (sec == only)
        pl.when(live)(functools.partial(stage, k))

    def step(i):
        pl.when(i == CHUNKS + 4)(lambda: loop(16, put_context))

        for lag, only, stage in stages:
            if lag is None:
                run(i >= 1, only, stage, 2 * i - 1)
                run(i >= 0, only, stage, 2 * i)
            else:
                k = i - lag
                run((k >= 0) & (i >= 0), only, stage, k)

    loop(CHUNKS + AHEAD + 2, step)


def local(boundary, context, weights, momentum, route, partner):
    beta = BETA_SCALE / math.sqrt(512)
    model = weights.shape[-1]
    width = model // CHUNKS
    n = CHUNKS
    dma = pltpu.SemaphoreType.DMA
    scratch = [
        pltpu.VMEM((8, 4, model), BF16),
        pltpu.VMEM((32, model), BF16),
        pltpu.VMEM((128, 4, 256), BF16),
        pltpu.VMEM((2, 256, 256), BF16),
        pltpu.VMEM((256, 512), BF16),
        pltpu.VMEM((512, 256), F32),
        pltpu.VMEM((n, 2, 8, 32, width), BF16),
        pltpu.VMEM((n, 2, 128, width), BF16),
        pltpu.VMEM((n, 2, 128, width), BF16),
        pltpu.VMEM((n, 2, 128, width), BF16),
        pltpu.VMEM((n, 2, 128, width), BF16),
        pltpu.VMEM((n, 8, 32, width), BF16),
        pltpu.VMEM((n, 8, 32, width), BF16),
        pltpu.VMEM((n, 8, 32, width), BF16),
        pltpu.VMEM((n, 32, width), F32),
        pltpu.VMEM((n, 4, 16, width), BF16),
        pltpu.VMEM((n, 4, 16, width), BF16),
        pltpu.VMEM((n, 4, 16, width), BF16),
        pltpu.VMEM((n, 2, 16, width), BF16),
        pltpu.VMEM((64, 32), BF16),
        pltpu.VMEM((32, 64), BF16),
        pltpu.VMEM((32, 128), F32),
        *[dma((n,))] * 17,
        dma((n, 2)),
        *[dma((n,))] * 2,
        *[dma] * 4,
    ]
    vmem = pl.BlockSpec(memory_space=pltpu.VMEM)
    smem = pl.BlockSpec(memory_space=pltpu.SMEM)
    anywhere = pl.BlockSpec(memory_space=pl.ANY)
    stream, ctx_grad, new_weights, new_momentum = pl.pallas_call(
        functools.partial(kernel, beta, width),
        out_shape=(
            pltpu.VMEM((8, 4, model), BF16),
            pltpu.VMEM((128, 4, 256), BF16),
            pltpu.VMEM((256, model), BF16),
            pltpu.VMEM((256, model), BF16),
        ),
        in_specs=[smem, smem, anywhere, anywhere, anywhere, anywhere],
        out_specs=(vmem, vmem, vmem, vmem),
        scratch_shapes=scratch,
        compiler_params=pltpu.CompilerParams(
            collective_id=0, has_side_effects=True, vmem_limit_bytes=50 * 2**20
        ),
        name="noloco_step",
    )(route.T, partner.T, boundary[0, 0], context[0, 0], weights[0, 0], momentum[0, 0])
    return stream[None, None], ctx_grad[None, None], new_weights[None, None], new_momentum[None, None]


def solution(mesh):
    in_specs = (
        P("replica", "section", "tensor", None, None),
        P("replica", "section", None, None, "tensor"),
        P("replica", "section", "tensor", None),
        P("replica", "section", "tensor", None),
        P(),
        P(),
    )
    out_specs = (
        P("replica", "section", "tensor", None, None),
        P("replica", "section", None, None, "tensor"),
        P("replica", "section", "tensor", None),
        P("replica", "section", "tensor", None),
    )
    return jax.shard_map(local, mesh=mesh, in_specs=in_specs, out_specs=out_specs, check_vma=False)
```
